32 devices in a mesh: fsdp: 2 (over y), ctx: 16 (over z, x, core).
Axes of the slice: x: 2, y: 2, z: 4, core: 2. Of those that a mesh axis runs over, the one named last changes fastest.
Arguments:
- block_input: bfloat16 [4096, 1088], P(('fsdp', 'ctx')), may hold values from -6 to 6
- cotangent: bfloat16 [4096, 1088], P(('fsdp', 'ctx')), may hold values from -6 to 6
- first_gain: bfloat16 [1088], P('fsdp'), may hold values from 0.5 to 1.5
- first_shift: bfloat16 [1088], P('fsdp'), may hold values from -3 to 3
- qkv_weight: bfloat16 [1088, 3264], P('fsdp'), may hold values from -0.1875 to 0.1875
- query_bias: bfloat16 [1088], P('fsdp'), may hold values from -3 to 3
- value_bias: bfloat16 [1088], P('fsdp'), may hold values from -3 to 3
- out_weight: bfloat16 [1088, 1088], P('fsdp'), may hold values from -1 to 1
- out_bias: bfloat16 [1088], P('fsdp'), may hold values from -3 to 3
- second_gain: bfloat16 [1088], P('fsdp'), may hold values from 0.5 to 1.5
- second_shift: bfloat16 [1088], P('fsdp'), may hold values from -3 to 3
- up_weight: bfloat16 [1088, 4352], P('fsdp'), may hold values from -0.1875 to 0.1875
- up_bias: bfloat16 [4352], P('fsdp'), may hold values from -3 to 3
- down_weight: bfloat16 [4352, 1088], P('fsdp'), may hold values from -0.09375 to 0.09375
- down_bias: bfloat16 [1088], P('fsdp'), may hold values from -3 to 3
Outputs:
- block_output: float32 [4096, 1088], P(('fsdp', 'ctx'))
- input_grad: float32 [4096, 1088], P(('fsdp', 'ctx'))
- grad_first_gain: float32 [1088], P('fsdp')
- grad_first_shift: float32 [1088], P('fsdp')
- grad_qkv: float32 [1088, 3264], P('fsdp')
- grad_query_bias: float32 [1088], P('fsdp')
- grad_value_bias: float32 [1088], P('fsdp')
- grad_out: float32 [1088, 1088], P('fsdp')
- grad_out_bias: float32 [1088], P('fsdp')
- grad_second_gain: float32 [1088], P('fsdp')
- grad_second_shift: float32 [1088], P('fsdp')
- grad_up: float32 [1088, 4352], P('fsdp')
- grad_up_bias: float32 [4352], P('fsdp')
- grad_down: float32 [4352, 1088], P('fsdp')
- grad_down_bias: float32 [1088], P('fsdp')
The draws below stay inside these ranges and needn't reach their ends.
All inputs are finite; a program needn't handle non-finite values.
Results may differ from the reference program's by a relative error of at most 0.025.
Values may be sent and summed in bfloat16 or wider, within the bound.
A program may use at most 192 MiB of HBM per device.

```python
import math
import jax
import jax.numpy as jnp
from jax import lax

HEADS = 17
HEAD_DIM = 64
FF = 4352
D = 1088
LENGTH = 2048
SEQS = 2
TOKENS = 4096


def levels(key, extent, pieces, smallest, top_value):
    factor_of, own = 1.0, jax.random.fold_in(key, 6)
    for dim, parts in pieces:
        heights = jnp.exp(jax.random.uniform(jax.random.fold_in(own, dim), (parts,), jnp.float32, smallest / len(pieces), top_value / len(pieces)))
        factor_of = factor_of * jnp.repeat(heights, extent[dim] // parts).reshape([-1 if axis == dim else 1 for axis in range(len(extent))])
    return factor_of


def centred(key, extent, deviation, bound, cuts=(), held_as=jnp.bfloat16):
    values = jax.random.normal(key, extent, jnp.float32) * deviation
    if len(cuts) > 0:
        values = levels(key, extent, cuts, -0.22, 0.18) * values
    return jnp.clip(values, min=-bound, max=bound).astype(held_as)


def setup_inputs(seed: int = 0) -> dict:
    seeds = jax.random.split(jax.random.key(seed), 16)
    block_input = centred(seeds[0], (TOKENS, D), 1.0, 6.0, ((0, 32),))
    cotangent = centred(seeds[1], (TOKENS, D), 1.0, 6.0, ((0, 32),))
    first_gain = jnp.clip(1.0 + 0.1 * jax.random.normal(seeds[2], (D,), jnp.float32), 0.5, 1.5).astype(jnp.bfloat16)
    first_shift = centred(seeds[3], (D,), 0.5, 3.0, ((0, 2),))
    qkv_weight = centred(seeds[4], (D, 3 * D), D ** -0.5, 0.1875, ((0, 2),))
    query_bias = centred(seeds[5], (D,), 0.5, 3.0, ((0, 2),))
    value_bias = centred(seeds[6], (D,), 0.5, 3.0, ((0, 2),))
    out_weight = centred(seeds[7], (D, D), (D // 32) ** -0.5, 1.0, ((0, 2),))
    out_bias = centred(seeds[8], (D,), 0.5, 3.0, ((0, 2),))
    second_gain = jnp.clip(1.0 + 0.1 * jax.random.normal(seeds[9], (D,), jnp.float32), 0.5, 1.5).astype(jnp.bfloat16)
    second_shift = centred(seeds[10], (D,), 0.5, 3.0, ((0, 2),))
    up_weight = centred(seeds[11], (D, FF), D ** -0.5, 0.1875, ((0, 2),))
    up_bias = centred(seeds[12], (FF,), 0.5, 3.0, ((0, 2),))
    down_weight = centred(seeds[13], (FF, D), FF ** -0.5, 0.09375, ((0, 2),))
    down_bias = centred(seeds[14], (D,), 0.5, 3.0, ((0, 2),))
    return {"block_input": block_input, "cotangent": cotangent, "first_gain": first_gain, "first_shift": first_shift, "qkv_weight": qkv_weight, "query_bias": query_bias, "value_bias": value_bias, "out_weight": out_weight, "out_bias": out_bias, "second_gain": second_gain, "second_shift": second_shift, "up_weight": up_weight, "up_bias": up_bias, "down_weight": down_weight, "down_bias": down_bias}


EPS = 1e-05
NEG = -1e+30

def normalize(rows, gain, shift):
    mean = lax.optimization_barrier(jnp.mean(rows, axis=-1, keepdims=True))
    centered = rows - mean
    rstd = lax.rsqrt(lax.optimization_barrier(jnp.mean(centered * centered, axis=-1, keepdims=True)) + EPS)
    hat = centered * rstd
    return (hat * gain.astype(jnp.float32) + shift.astype(jnp.float32), hat, rstd)

def normalize_back(grad, hat, rstd, gain):
    scaled = grad * gain.astype(jnp.float32)
    return rstd * (scaled - lax.optimization_barrier(jnp.mean(scaled, axis=-1, keepdims=True)) - hat * lax.optimization_barrier(jnp.mean(scaled * hat, axis=-1, keepdims=True)))

def gelu_tanh(value):
    return jax.nn.gelu(value, approximate=True)

def gelu_back(pre, grad):
    _, pull = jax.vjp(gelu_tanh, pre)
    return pull(grad)[0]

def contract(left, right, left_dim, right_dim):
    return lax.dot_general(left, right, (((left_dim,), (right_dim,)), ((), ())), preferred_element_type=jnp.float32)

def masked_scores(query_rows, keys, start, rows_block, scale):
    scores = jnp.einsum('bhe,khe->hbk', query_rows.astype(jnp.float32), keys.astype(jnp.float32)) * scale
    query_pos = start + jnp.arange(rows_block, dtype=jnp.int32)
    key_pos = jnp.arange(keys.shape[0], dtype=jnp.int32)
    allowed = key_pos[None, None, :] <= query_pos[None, :, None]
    return jnp.where(allowed, scores, NEG)

def attention_forward(query, keys, values):
    length = query.shape[0]
    rows_block = math.gcd(512, length)
    scale = HEAD_DIM ** (-0.5)

    def one_block(start):
        query_rows = lax.dynamic_slice_in_dim(query, start, rows_block, 0)
        scores = masked_scores(query_rows, keys, start, rows_block, scale)
        row_max = lax.optimization_barrier(jnp.max(scores, axis=-1, keepdims=True))
        weights = jnp.exp(scores - row_max)
        total = lax.optimization_barrier(jnp.sum(weights, axis=-1, keepdims=True))
        mixed = jnp.einsum('hbk,khe->hbe', weights.astype(jnp.bfloat16).astype(jnp.float32), values.astype(jnp.float32)) / total
        return (mixed.transpose(1, 0, 2).astype(jnp.bfloat16), (row_max + jnp.log(total))[:, :, 0].T)
    starts = jnp.arange(length // rows_block, dtype=jnp.int32) * rows_block
    attended, lse = lax.map(one_block, starts)
    return (attended.reshape(query.shape), lse.reshape(length, HEADS))

def attention_backward(query, keys, values, attended, lse, grad_attended):
    length = query.shape[0]
    rows_block = math.gcd(512, length)
    scale = HEAD_DIM ** (-0.5)
    delta = lax.optimization_barrier(jnp.sum(grad_attended.astype(jnp.float32) * attended.astype(jnp.float32), axis=-1))

    def one_block(carry, start):
        grad_keys, grad_values = carry
        query_rows = lax.dynamic_slice_in_dim(query, start, rows_block, 0)
        grad_rows = lax.dynamic_slice_in_dim(grad_attended, start, rows_block, 0).astype(jnp.float32)
        lse_rows = lax.dynamic_slice_in_dim(lse, start, rows_block, 0)
        delta_rows = lax.dynamic_slice_in_dim(delta, start, rows_block, 0)
        scores = masked_scores(query_rows, keys, start, rows_block, scale)
        prob = jnp.exp(scores - lse_rows.T[:, :, None])
        grad_values = grad_values + jnp.einsum('hbk,bhe->khe', prob.astype(jnp.bfloat16).astype(jnp.float32), grad_rows)
        grad_prob = jnp.einsum('bhe,khe->hbk', grad_rows, values.astype(jnp.float32))
        grad_score = (prob * (grad_prob - delta_rows.T[:, :, None]) * scale).astype(jnp.bfloat16).astype(jnp.float32)
        grad_query_rows = jnp.einsum('hbk,khe->bhe', grad_score, keys.astype(jnp.float32))
        grad_keys = grad_keys + jnp.einsum('hbk,bhe->khe', grad_score, query_rows.astype(jnp.float32))
        return ((grad_keys, grad_values), grad_query_rows)
    zeros = jnp.zeros(query.shape, jnp.float32)
    starts = jnp.arange(length // rows_block, dtype=jnp.int32) * rows_block
    (grad_keys, grad_values), grad_query = lax.scan(one_block, (zeros, zeros), starts)
    return (grad_query.reshape(query.shape), grad_keys, grad_values)

def one_sequence(rows_in, cot_rows, params):
    first_gain, first_shift, qkv_weight, query_bias, value_bias, out_weight, out_bias, second_gain, second_shift, up_weight, up_bias, down_weight, down_bias = params
    rows = rows_in.astype(jnp.float32)
    first_norm, first_hat, first_rstd = normalize(rows, first_gain, first_shift)
    first_act = first_norm.astype(jnp.bfloat16)
    qkv = jnp.dot(first_act, qkv_weight, preferred_element_type=jnp.float32)
    shape_heads = (rows.shape[0], HEADS, HEAD_DIM)
    query = (qkv[:, :D] + query_bias.astype(jnp.float32)).astype(jnp.bfloat16).reshape(shape_heads)
    keys = qkv[:, D:2 * D].astype(jnp.bfloat16).reshape(shape_heads)
    values = (qkv[:, 2 * D:] + value_bias.astype(jnp.float32)).astype(jnp.bfloat16).reshape(shape_heads)
    attended, lse = attention_forward(query, keys, values)
    joined = attended.reshape(rows.shape[0], D)
    mid = rows + jnp.dot(joined, out_weight, preferred_element_type=jnp.float32) + out_bias.astype(jnp.float32)
    second_norm, second_hat, second_rstd = normalize(mid, second_gain, second_shift)
    second_act = second_norm.astype(jnp.bfloat16)
    pre = jnp.dot(second_act, up_weight, preferred_element_type=jnp.float32) + up_bias.astype(jnp.float32)
    act = gelu_tanh(pre).astype(jnp.bfloat16)
    output = mid + jnp.dot(act, down_weight, preferred_element_type=jnp.float32) + down_bias.astype(jnp.float32)
    cot_float = cot_rows.astype(jnp.float32)
    grad_down = contract(act, cot_rows, 0, 0)
    grad_down_bias = lax.optimization_barrier(jnp.sum(cot_float, axis=0))
    grad_pre = gelu_back(pre, contract(cot_rows, down_weight, 1, 1))
    grad_pre_b = grad_pre.astype(jnp.bfloat16)
    grad_up = contract(second_act, grad_pre_b, 0, 0)
    grad_up_bias = lax.optimization_barrier(jnp.sum(grad_pre, axis=0))
    grad_second = contract(grad_pre_b, up_weight, 1, 1)
    grad_second_gain = lax.optimization_barrier(jnp.sum(grad_second * second_hat, axis=0))
    grad_second_shift = lax.optimization_barrier(jnp.sum(grad_second, axis=0))
    grad_mid = cot_float + normalize_back(grad_second, second_hat, second_rstd, second_gain)
    grad_mid_b = grad_mid.astype(jnp.bfloat16)
    grad_out = contract(joined, grad_mid_b, 0, 0)
    grad_out_bias = lax.optimization_barrier(jnp.sum(grad_mid, axis=0))
    grad_attended = contract(grad_mid_b, out_weight, 1, 1).astype(jnp.bfloat16).reshape(shape_heads)
    grad_query, grad_keys, grad_values = attention_backward(query, keys, values, attended, lse, grad_attended)
    grad_query = grad_query.reshape(rows.shape[0], D)
    grad_keys = grad_keys.reshape(rows.shape[0], D)
    grad_values = grad_values.reshape(rows.shape[0], D)
    grad_query_bias = lax.optimization_barrier(jnp.sum(grad_query, axis=0))
    grad_value_bias = lax.optimization_barrier(jnp.sum(grad_values, axis=0))
    grad_qkv_b = jnp.concatenate([grad_query, grad_keys, grad_values], axis=1).astype(jnp.bfloat16)
    grad_qkv = contract(first_act, grad_qkv_b, 0, 0)
    grad_first = contract(grad_qkv_b, qkv_weight, 1, 1)
    grad_first_gain = lax.optimization_barrier(jnp.sum(grad_first * first_hat, axis=0))
    grad_first_shift = lax.optimization_barrier(jnp.sum(grad_first, axis=0))
    input_grad = grad_mid + normalize_back(grad_first, first_hat, first_rstd, first_gain)
    grads = (grad_first_gain, grad_first_shift, grad_qkv, grad_query_bias, grad_value_bias, grad_out, grad_out_bias, grad_second_gain, grad_second_shift, grad_up, grad_up_bias, grad_down, grad_down_bias)
    return (output, input_grad, grads)

def reference(block_input, cotangent, first_gain, first_shift, qkv_weight, query_bias, value_bias, out_weight, out_bias, second_gain, second_shift, up_weight, up_bias, down_weight, down_bias):
    params = (first_gain, first_shift, qkv_weight, query_bias, value_bias, out_weight, out_bias, second_gain, second_shift, up_weight, up_bias, down_weight, down_bias)
    inputs = block_input.reshape(SEQS, LENGTH, D)
    cots = cotangent.reshape(SEQS, LENGTH, D)
    start = tuple((jnp.zeros(param.shape, jnp.float32) for param in params))

    def step(totals, data):
        output, input_grad, grads = one_sequence(data[0], data[1], params)
        return (tuple((total + grad for total, grad in zip(totals, grads))), (output, input_grad))
    totals, (outputs, input_grads) = lax.scan(step, start, (inputs, cots))
    return (outputs.reshape(TOKENS, D), input_grads.reshape(TOKENS, D), totals[0], totals[1], totals[2], totals[3], totals[4], totals[5], totals[6], totals[7], totals[8], totals[9], totals[10], totals[11], totals[12])
```

```python
import jax
import jax.numpy as jnp
from jax import lax
from jax.experimental import pallas as pl
from jax.experimental.pallas import tpu as pltpu
from jax.sharding import PartitionSpec as P

HEADS = 17
HEAD_DIM = 64


EPS = 1e-05
NEG = -1e30


def shifted(block, axis, distance):
    devices = range(lax.axis_size(axis))
    route = [(i - distance, i) for i in devices if i - distance in devices]
    return lax.ppermute(block, axis, route)


def from_behind(value, axis, steps):
    count = lax.axis_size(axis)
    pairs = [(source, (source + steps) % count) for source in range(count)]
    return lax.ppermute(value, axis, pairs)


def normalize(rows, gain, shift):
    mean = jnp.mean(rows, axis=-1, keepdims=True)
    centered = rows - mean
    rstd = lax.rsqrt(jnp.mean(centered * centered, axis=-1, keepdims=True) + EPS)
    hat = centered * rstd
    return (hat * gain + shift, hat, rstd)


def normalize_back(grad, hat, rstd, gain):
    scaled = grad * gain
    return rstd * (
        scaled
        - jnp.mean(scaled, axis=-1, keepdims=True)
        - hat * jnp.mean(scaled * hat, axis=-1, keepdims=True)
    )


def gelu_tanh(value):
    return jax.nn.gelu(value, approximate=True)


def gelu_back(pre, grad):
    _, pull = jax.vjp(gelu_tanh, pre)
    return pull(grad)[0]


def contract(left, right, left_dim, right_dim):
    return lax.dot_general(
        left, right, (((left_dim,), (right_dim,)), ((), ())), preferred_element_type=jnp.float32
    )


def block_scores(query, key_block, query_pos, key_pos, scale):
    scores = (
        jnp.einsum("the,khe->htk", query, key_block, preferred_element_type=jnp.float32) * scale
    )
    allowed = key_pos[None, None, :] <= query_pos[None, :, None]
    return jnp.where(allowed, scores, NEG)


def matmul(left, right, left_dim, right_dim):
    return lax.dot_general(
        left, right, (((left_dim,), (right_dim,)), ((), ())), preferred_element_type=jnp.float32
    )


QUERY_ROWS = 256


def softmax_block(query, keys, values, first_query):
    scores = matmul(keys, query, 1, 1)
    key_pos = lax.broadcasted_iota(jnp.int32, scores.shape, 0)
    query_pos = lax.broadcasted_iota(jnp.int32, scores.shape, 1) + first_query
    scores = jnp.where(key_pos <= query_pos, scores, NEG)
    top = jnp.max(scores, axis=0, keepdims=True)
    weights = jnp.exp(scores - top)
    total = jnp.sum(weights, axis=0, keepdims=True)
    mixed = matmul(values, weights.astype(jnp.bfloat16), 0, 0) / total
    return mixed.astype(jnp.bfloat16), top + jnp.log(total)


def attend_kernel(place_ref, packed_ref, extra_ref, out_ref, outt_ref, lse_ref, xout_ref, xoutt_ref, xlse_ref):
    length = packed_ref.shape[0]
    scale = HEAD_DIM ** (-0.5)
    for start in range(0, length, QUERY_ROWS):
        stop = start + QUERY_ROWS
        query = packed_ref[start:stop, 0:64] * scale
        mixed, lse = softmax_block(
            query.astype(jnp.bfloat16), packed_ref[0:stop, 64:128], packed_ref[0:stop, 128:192], start
        )
        outt_ref[:, start:stop] = mixed
        out_ref[start:stop, :] = mixed.astype(jnp.float32).T.astype(jnp.bfloat16)
        lse_ref[:, start:stop] = lse
    query = (extra_ref[...] * scale).astype(jnp.bfloat16)
    mixed, lse = softmax_block(
        query, packed_ref[:, 192:256], packed_ref[:, 256:320], place_ref[0] * extra_ref.shape[0]
    )
    xoutt_ref[...] = mixed
    xout_ref[...] = mixed.astype(jnp.float32).T.astype(jnp.bfloat16)
    xlse_ref[...] = lse


def back_block(query, keys, values, lse, grad, mixed, first_query):
    scale = HEAD_DIM ** (-0.5)
    query = (query * scale).astype(jnp.bfloat16)
    scores = matmul(keys, query, 1, 1)
    key_pos = lax.broadcasted_iota(jnp.int32, scores.shape, 0)
    query_pos = lax.broadcasted_iota(jnp.int32, scores.shape, 1) + first_query
    prob = jnp.where(key_pos <= query_pos, jnp.exp(scores - lse), 0.0)
    grad_values = matmul(prob.astype(jnp.bfloat16), grad, 1, 0)
    grad_prob = matmul(values, grad, 1, 1)
    delta = jnp.sum(
        grad.astype(jnp.float32).T * mixed.astype(jnp.float32), axis=0, keepdims=True
    )
    grad_score = (prob * (grad_prob - delta)).astype(jnp.bfloat16)
    grad_keys = matmul(grad_score, query, 1, 0)
    grad_query = matmul(keys, grad_score, 0, 0) * scale
    return grad_query.T, grad_keys, grad_values


def attend_back_kernel(
    place_ref, packed_ref, extra_ref, outt_ref, lse_ref, xoutt_ref, xlse_ref, grad_ref, xgrad_ref,
    dpacked_ref, dextra_ref, dkeys, dvalues,
):
    length = packed_ref.shape[0]
    starts = list(range(0, length, QUERY_ROWS))
    for start in reversed(starts):
        stop = start + QUERY_ROWS
        dq, dk, dv = back_block(
            packed_ref[start:stop, 0:64], packed_ref[0:stop, 64:128], packed_ref[0:stop, 128:192],
            lse_ref[:, start:stop], grad_ref[start:stop, :], outt_ref[:, start:stop], start,
        )
        dpacked_ref[start:stop, 0:64] = dq.astype(jnp.bfloat16)
        if start == starts[-1]:
            dkeys[...] = dk
            dvalues[...] = dv
        else:
            dkeys[0:stop, :] += dk
            dvalues[0:stop, :] += dv
    dpacked_ref[:, 64:128] = dkeys[...].astype(jnp.bfloat16)
    dpacked_ref[:, 128:192] = dvalues[...].astype(jnp.bfloat16)
    dq, dk, dv = back_block(
        extra_ref[...], packed_ref[:, 192:256], packed_ref[:, 256:320],
        xlse_ref[...], xgrad_ref[...], xoutt_ref[...], place_ref[0] * extra_ref.shape[0],
    )
    dextra_ref[...] = dq.astype(jnp.bfloat16)
    dpacked_ref[:, 192:256] = dk.astype(jnp.bfloat16)
    dpacked_ref[:, 256:320] = dv.astype(jnp.bfloat16)


def vmem(count):
    return [pl.BlockSpec(memory_space=pltpu.VMEM)] * count


def attend(place, packed, extra):
    length, rows = packed.shape[0], extra.shape[0]
    bf16, f32 = jnp.bfloat16, jnp.float32
    return pl.pallas_call(
        attend_kernel,
        out_shape=(
            jax.ShapeDtypeStruct((length, HEAD_DIM), bf16),
            jax.ShapeDtypeStruct((HEAD_DIM, length), bf16),
            jax.ShapeDtypeStruct((1, length), f32),
            jax.ShapeDtypeStruct((rows, HEAD_DIM), bf16),
            jax.ShapeDtypeStruct((HEAD_DIM, rows), bf16),
            jax.ShapeDtypeStruct((1, rows), f32),
        ),
        in_specs=[pl.BlockSpec(memory_space=pltpu.SMEM)] + vmem(2),
        out_specs=tuple(vmem(6)),
        compiler_params=pltpu.CompilerParams(vmem_limit_bytes=40 * 2**20),
        name="attend",
    )(place, packed, extra)


def attend_back(place, packed, extra, outt, lse, xoutt, xlse, grad, xgrad):
    length, rows = packed.shape[0], extra.shape[0]
    return pl.pallas_call(
        attend_back_kernel,
        out_shape=(
            jax.ShapeDtypeStruct((length, 5 * HEAD_DIM), jnp.bfloat16),
            jax.ShapeDtypeStruct((rows, HEAD_DIM), jnp.bfloat16),
        ),
        in_specs=[pl.BlockSpec(memory_space=pltpu.SMEM)] + vmem(8),
        out_specs=tuple(vmem(2)),
        scratch_shapes=[
            pltpu.VMEM((length, HEAD_DIM), jnp.float32),
            pltpu.VMEM((length, HEAD_DIM), jnp.float32),
        ],
        compiler_params=pltpu.CompilerParams(vmem_limit_bytes=48 * 2**20),
        name="attend_back",
    )(place, packed, extra, outt, lse, xoutt, xlse, grad, xgrad)


def swap(blocks_of, axis):
    return lax.all_to_all(blocks_of, axis, split_axis=0, concat_axis=0, tiled=True)


def by_head(rows_of, blocks):
    return rows_of[:, : blocks * HEAD_DIM].reshape(-1, blocks, HEAD_DIM).transpose(1, 0, 2)


def from_head(parts, last):
    blocks, rows, _ = parts.shape
    return jnp.concatenate([parts.transpose(1, 0, 2).reshape(rows, blocks * HEAD_DIM), last], axis=1)


def head_attention(query, keys, values):
    blocks = lax.axis_size("ctx")
    rows = query.shape[0]
    place = lax.axis_index("ctx").astype(jnp.int32).reshape(1)
    cut = blocks * HEAD_DIM
    shared = jnp.concatenate([keys[:, cut:], values[:, cut:]], axis=1)
    packed = jnp.concatenate(
        [by_head(query, blocks), by_head(keys, blocks), by_head(values, blocks),
         jnp.broadcast_to(shared[None], (blocks, rows, 2 * HEAD_DIM))],
        axis=2,
    )
    packed = swap(packed, "ctx").reshape(blocks * rows, 5 * HEAD_DIM)
    extra = query[:, cut:]
    out, outt, lse, xout, xoutt, xlse = attend(place, packed, extra)
    back = swap(out.reshape(blocks, rows, HEAD_DIM), "ctx")
    joined = from_head(back, xout)

    def backward(grad_joined):
        grad = swap(by_head(grad_joined, blocks), "ctx").reshape(blocks * rows, HEAD_DIM)
        dpacked, dextra = attend_back(
            place, packed, extra, outt, lse, xoutt, xlse, grad, grad_joined[:, cut:]
        )
        dback = swap(dpacked.reshape(blocks, rows, 5 * HEAD_DIM), "ctx")
        dshared = jnp.sum(dback[:, :, 3 * HEAD_DIM :].astype(jnp.float32), axis=0).astype(jnp.bfloat16)
        return (
            from_head(dback[:, :, :HEAD_DIM], dextra),
            from_head(dback[:, :, HEAD_DIM : 2 * HEAD_DIM], dshared[:, :HEAD_DIM]),
            from_head(dback[:, :, 2 * HEAD_DIM : 3 * HEAD_DIM], dshared[:, HEAD_DIM:]),
        )

    return joined, backward


def ring_attention(query, keys, values):
    position = lax.axis_index("ctx")
    blocks = lax.axis_size("ctx")
    count_rows, width = query.shape
    scale = HEAD_DIM ** (-0.5)
    offsets = jnp.arange(count_rows, dtype=jnp.int32)
    query_pos = position * count_rows + offsets
    shape_heads = (count_rows, HEADS, HEAD_DIM)
    query, keys, values = (part.reshape(shape_heads) for part in (query, keys, values))

    def forward_block(carry, key_block, value_block, source):
        run_max, run_sum, accum = carry
        scores = block_scores(query, key_block, query_pos, source * count_rows + offsets, scale)
        new_max = jnp.maximum(run_max, jnp.max(scores, axis=-1))
        factor = jnp.exp(run_max - new_max)
        weights = jnp.exp(scores - new_max[:, :, None])
        run_sum = run_sum * factor + jnp.sum(weights, axis=-1)
        accum = accum * factor[:, :, None] + jnp.einsum(
            "htk,khe->hte",
            weights.astype(jnp.bfloat16),
            value_block,
            preferred_element_type=jnp.float32,
        )
        return (new_max, run_sum, accum)

    def forward_visit(step, state):
        carry, key_block, value_block, stored = state
        source = (position - step) % blocks
        carry = lax.cond(
            source <= position,
            lambda inner: forward_block(inner, key_block, value_block, source),
            lambda inner: inner,
            carry,
        )
        return (carry, key_block, value_block, stored)

    def forward_step(step, state):
        carry, key_block, value_block, stored = forward_visit(step, state)
        key_block, value_block = shifted((key_block, value_block), "ctx", 1)
        return (carry, key_block, value_block, stored)

    stored_start = ()
    start = (
        jnp.full((HEADS, count_rows), NEG, jnp.float32),
        jnp.zeros((HEADS, count_rows), jnp.float32),
        jnp.zeros((HEADS, count_rows, HEAD_DIM), jnp.float32),
    )
    state = lax.fori_loop(0, blocks - 1, forward_step, (start, keys, values, stored_start))
    (run_max, run_sum, accum), _, _, stored_blocks = forward_visit(blocks - 1, state)
    attended = (accum / run_sum[:, :, None]).transpose(1, 0, 2).astype(jnp.bfloat16)
    lse = run_max + jnp.log(run_sum)

    def backward(grad_joined):
        grad_attended = grad_joined.reshape(shape_heads)
        delta_rows = jnp.sum(
            grad_attended.astype(jnp.float32) * attended.astype(jnp.float32), axis=-1
        ).T

        def backward_block(source, key_block, value_block, grads):
            grad_query, grad_keys, grad_values = grads
            scores = block_scores(query, key_block, query_pos, source * count_rows + offsets, scale)
            prob = jnp.exp(scores - lse[:, :, None])
            grad_values = grad_values + jnp.einsum(
                "htk,the->khe",
                prob.astype(jnp.bfloat16),
                grad_attended,
                preferred_element_type=jnp.float32,
            )
            grad_prob = jnp.einsum(
                "the,khe->htk", grad_attended, value_block, preferred_element_type=jnp.float32
            )
            grad_score = (prob * (grad_prob - delta_rows[:, :, None]) * scale).astype(jnp.bfloat16)
            grad_query = grad_query + jnp.einsum(
                "htk,khe->the", grad_score, key_block, preferred_element_type=jnp.float32
            )
            grad_keys = grad_keys + jnp.einsum(
                "htk,the->khe", grad_score, query, preferred_element_type=jnp.float32
            )
            return (grad_query, grad_keys, grad_values)

        zero_block = jnp.zeros(shape_heads, jnp.float32)

        def backward_step(step, state):
            grad_query, key_block, value_block, grad_keys, grad_values = state
            source = (position - step) % blocks
            grad_query, grad_keys, grad_values = lax.cond(
                source <= position,
                lambda inner: backward_block(source, key_block, value_block, inner),
                lambda inner: inner,
                (grad_query, grad_keys, grad_values),
            )
            key_block, value_block = shifted((key_block, value_block), "ctx", 1)
            grad_keys, grad_values = from_behind((grad_keys, grad_values), "ctx", 1)
            return (grad_query, key_block, value_block, grad_keys, grad_values)

        grad_query, _, _, grad_keys, grad_values = lax.fori_loop(
            0, blocks, backward_step, (zero_block, keys, values, zero_block, zero_block)
        )
        return tuple(
            part.reshape(count_rows, width) for part in (grad_query, grad_keys, grad_values)
        )

    return attended.reshape(count_rows, width), backward


def on_device(
    block_input,
    cotangent,
    first_gain,
    first_shift,
    qkv_weight,
    query_bias,
    value_bias,
    out_weight,
    out_bias,
    second_gain,
    second_shift,
    up_weight,
    up_bias,
    down_weight,
    down_bias,
):
    fsdp = lax.axis_size("fsdp")
    blocks = lax.axis_size("ctx")
    place = lax.axis_index("fsdp")
    width = HEADS * HEAD_DIM
    f32, bf16 = jnp.float32, jnp.bfloat16
    small = (
        first_gain, first_shift, query_bias, value_bias, out_bias, second_gain, second_shift,
        down_bias, up_bias,
    )
    sizes = [part.shape[0] for part in small]
    gathered = lax.all_gather(jnp.concatenate(small), "fsdp", axis=0, tiled=False)
    whole_small, at = [], 0
    for size in sizes:
        whole_small.append(gathered[:, at : at + size].reshape(fsdp * size).astype(f32))
        at += size
    gain_one, shift_one, bias_q, bias_v, bias_o, gain_two, shift_two, bias_d, bias_u = whole_small
    whole_qkv, whole_out, whole_up, whole_down = (
        lax.all_gather(part, "fsdp", axis=0, tiled=True)
        for part in (qkv_weight, out_weight, up_weight, down_weight)
    )
    rows = block_input.astype(f32)
    first_norm, first_hat, first_rstd = normalize(rows, gain_one, shift_one)
    first_act = first_norm.astype(bf16)
    qkv = jnp.dot(first_act, whole_qkv, preferred_element_type=f32)
    query = (qkv[:, :width] + bias_q).astype(bf16)
    keys = qkv[:, width : 2 * width].astype(bf16)
    values = (qkv[:, 2 * width :] + bias_v).astype(bf16)
    attention = head_attention if HEADS == blocks + 1 else ring_attention
    joined, attention_back = attention(query, keys, values)
    mid = rows + jnp.dot(joined, whole_out, preferred_element_type=f32) + bias_o
    second_norm, second_hat, second_rstd = normalize(mid, gain_two, shift_two)
    second_act = second_norm.astype(bf16)
    pre = jnp.dot(second_act, whole_up, preferred_element_type=f32) + bias_u
    act = gelu_tanh(pre).astype(bf16)
    block_output = mid + jnp.dot(act, whole_down, preferred_element_type=f32) + bias_d

    def left(part):
        return lax.all_to_all(part, "fsdp", split_axis=1, concat_axis=0, tiled=True)

    def right(part):
        return lax.all_gather(part, "fsdp", axis=0, tiled=True)

    def weight_grad(left_part, right_part):
        return lax.psum(contract(left(left_part), right(right_part), 0, 0).astype(bf16), "ctx")

    cot_float = cotangent.astype(f32)
    grad_down = weight_grad(act, cotangent)
    grad_down_bias = jnp.sum(cot_float, axis=0)
    grad_pre = gelu_back(pre, contract(cotangent, whole_down, 1, 1))
    grad_pre_b = grad_pre.astype(bf16)
    grad_up = weight_grad(second_act, grad_pre_b)
    grad_up_bias = jnp.sum(grad_pre, axis=0)
    grad_second = contract(grad_pre_b, whole_up, 1, 1)
    grad_second_gain = jnp.sum(grad_second * second_hat, axis=0)
    grad_second_shift = jnp.sum(grad_second, axis=0)
    grad_mid = cot_float + normalize_back(grad_second, second_hat, second_rstd, gain_two)
    grad_mid_b = grad_mid.astype(bf16)
    grad_out = weight_grad(joined, grad_mid_b)
    grad_out_bias = jnp.sum(grad_mid, axis=0)
    grad_attended = contract(grad_mid_b, whole_out, 1, 1).astype(bf16)
    grad_query, grad_keys, grad_values = attention_back(grad_attended)
    grad_query_bias = jnp.sum(grad_query.astype(f32), axis=0)
    grad_value_bias = jnp.sum(grad_values.astype(f32), axis=0)
    grad_qkv_b = jnp.concatenate([grad_query, grad_keys, grad_values], axis=1).astype(bf16)
    grad_qkv = weight_grad(first_act, grad_qkv_b)
    grad_first = contract(grad_qkv_b, whole_qkv, 1, 1)
    grad_first_gain = jnp.sum(grad_first * first_hat, axis=0)
    grad_first_shift = jnp.sum(grad_first, axis=0)
    input_grad = grad_mid + normalize_back(grad_first, first_hat, first_rstd, gain_one)
    vectors = (
        grad_first_gain, grad_first_shift, grad_query_bias, grad_value_bias, grad_out_bias,
        grad_second_gain, grad_second_shift, grad_down_bias, grad_up_bias,
    )
    summed = lax.psum(
        jnp.concatenate([part.reshape(fsdp, -1) for part in vectors], axis=1), ("fsdp", "ctx")
    )
    mine = lax.dynamic_index_in_dim(summed, place, 0, keepdims=False)
    shards, at = [], 0
    for size in sizes:
        shards.append(mine[at : at + size])
        at += size
    gain_g1, shift_g1, bias_gq, bias_gv, bias_go, gain_g2, shift_g2, bias_gd, bias_gu = shards
    return (
        block_output,
        input_grad,
        gain_g1,
        shift_g1,
        grad_qkv.astype(f32),
        bias_gq,
        bias_gv,
        grad_out.astype(f32),
        bias_go,
        gain_g2,
        shift_g2,
        grad_up.astype(f32),
        bias_gu,
        grad_down.astype(f32),
        bias_gd,
    )


def solution(mesh):
    placed = (
        P(("fsdp", "ctx"), None),
        P(("fsdp", "ctx"), None),
        P("fsdp"),
        P("fsdp"),
        P("fsdp", None),
        P("fsdp"),
        P("fsdp"),
        P("fsdp", None),
        P("fsdp"),
        P("fsdp"),
        P("fsdp"),
        P("fsdp", None),
        P("fsdp"),
        P("fsdp", None),
        P("fsdp"),
    )
    return jax.shard_map(
        on_device,
        mesh=mesh,
        in_specs=placed,
        out_specs=(
            P(("fsdp", "ctx"), None),
            P(("fsdp", "ctx"), None),
            P("fsdp"),
            P("fsdp"),
            P("fsdp", None),
            P("fsdp"),
            P("fsdp"),
            P("fsdp", None),
            P("fsdp"),
            P("fsdp"),
            P("fsdp"),
            P("fsdp", None),
            P("fsdp"),
            P("fsdp", None),
            P("fsdp"),
        ),
        check_vma=False,
    )
```

```python
import jax
import jax.numpy as jnp
from jax import lax
from jax.experimental import pallas as pl
from jax.experimental.pallas import tpu as pltpu
from jax.sharding import PartitionSpec as P

HEADS = 17
HEAD_DIM = 64


EPS = 1e-05
NEG = -1e30


def shifted(block, axis, distance):
    devices = range(lax.axis_size(axis))
    route = [(i - distance, i) for i in devices if i - distance in devices]
    return lax.ppermute(block, axis, route)


def from_behind(value, axis, steps):
    count = lax.axis_size(axis)
    pairs = [(source, (source + steps) % count) for source in range(count)]
    return lax.ppermute(value, axis, pairs)


def normalize(rows, gain, shift):
    mean = jnp.mean(rows, axis=-1, keepdims=True)
    centered = rows - mean
    rstd = lax.rsqrt(jnp.mean(centered * centered, axis=-1, keepdims=True) + EPS)
    hat = centered * rstd
    return (hat * gain + shift, hat, rstd)


def normalize_back(grad, hat, rstd, gain):
    scaled = grad * gain
    return rstd * (
        scaled
        - jnp.mean(scaled, axis=-1, keepdims=True)
        - hat * jnp.mean(scaled * hat, axis=-1, keepdims=True)
    )


def gelu_tanh(value):
    return jax.nn.gelu(value, approximate=True)


def gelu_back(pre, grad):
    _, pull = jax.vjp(gelu_tanh, pre)
    return pull(grad)[0]


def contract(left, right, left_dim, right_dim):
    return lax.dot_general(
        left, right, (((left_dim,), (right_dim,)), ((), ())), preferred_element_type=jnp.float32
    )


def block_scores(query, key_block, query_pos, key_pos, scale):
    scores = (
        jnp.einsum("the,khe->htk", query, key_block, preferred_element_type=jnp.float32) * scale
    )
    allowed = key_pos[None, None, :] <= query_pos[None, :, None]
    return jnp.where(allowed, scores, NEG)


def matmul(left, right, left_dim, right_dim):
    return lax.dot_general(
        left, right, (((left_dim,), (right_dim,)), ((), ())), preferred_element_type=jnp.float32
    )


QUERY_ROWS = 256


def softmax_block(query, keys, values, first_query):
    scores = matmul(keys, query, 1, 1)
    key_pos = lax.broadcasted_iota(jnp.int32, scores.shape, 0)
    query_pos = lax.broadcasted_iota(jnp.int32, scores.shape, 1) + first_query
    scores = jnp.where(key_pos <= query_pos, scores, NEG)
    top = jnp.max(scores, axis=0, keepdims=True)
    weights = jnp.exp(scores - top)
    total = jnp.sum(weights, axis=0, keepdims=True)
    mixed = matmul(values, weights.astype(jnp.bfloat16), 0, 0) / total
    return mixed.astype(jnp.bfloat16), top + jnp.log(total)


def attend_kernel(place_ref, packed_ref, extra_ref, out_ref, outt_ref, lse_ref, xout_ref, xoutt_ref, xlse_ref):
    length = packed_ref.shape[0]
    scale = HEAD_DIM ** (-0.5)
    for start in range(0, length, QUERY_ROWS):
        stop = start + QUERY_ROWS
        query = packed_ref[start:stop, 0:64] * scale
        mixed, lse = softmax_block(
            query.astype(jnp.bfloat16), packed_ref[0:stop, 64:128], packed_ref[0:stop, 128:192], start
        )
        outt_ref[:, start:stop] = mixed
        out_ref[start:stop, :] = mixed.astype(jnp.float32).T.astype(jnp.bfloat16)
        lse_ref[:, start:stop] = lse
    query = (extra_ref[...] * scale).astype(jnp.bfloat16)
    mixed, lse = softmax_block(
        query, packed_ref[:, 192:256], packed_ref[:, 256:320], place_ref[0] * extra_ref.shape[0]
    )
    xoutt_ref[...] = mixed
    xout_ref[...] = mixed.astype(jnp.float32).T.astype(jnp.bfloat16)
    xlse_ref[...] = lse


def back_block(query, keys, values, lse, grad, mixed, first_query):
    scale = HEAD_DIM ** (-0.5)
    query = (query * scale).astype(jnp.bfloat16)
    scores = matmul(keys, query, 1, 1)
    key_pos = lax.broadcasted_iota(jnp.int32, scores.shape, 0)
    query_pos = lax.broadcasted_iota(jnp.int32, scores.shape, 1) + first_query
    prob = jnp.where(key_pos <= query_pos, jnp.exp(scores - lse), 0.0)
    grad_values = matmul(prob.astype(jnp.bfloat16), grad, 1, 0)
    grad_prob = matmul(values, grad, 1, 1)
    delta = jnp.sum(
        grad.astype(jnp.float32).T * mixed.astype(jnp.float32), axis=0, keepdims=True
    )
    grad_score = (prob * (grad_prob - delta)).astype(jnp.bfloat16)
    grad_keys = matmul(grad_score, query, 1, 0)
    grad_query = matmul(keys, grad_score, 0, 0) * scale
    return grad_query.T, grad_keys, grad_values


def attend_back_kernel(
    place_ref, packed_ref, extra_ref, outt_ref, lse_ref, xoutt_ref, xlse_ref, grad_ref, xgrad_ref,
    dpacked_ref, dextra_ref, dkeys, dvalues,
):
    length = packed_ref.shape[0]
    starts = list(range(0, length, QUERY_ROWS))
    for start in reversed(starts):
        stop = start + QUERY_ROWS
        dq, dk, dv = back_block(
            packed_ref[start:stop, 0:64], packed_ref[0:stop, 64:128], packed_ref[0:stop, 128:192],
            lse_ref[:, start:stop], grad_ref[start:stop, :], outt_ref[:, start:stop], start,
        )
        dpacked_ref[start:stop, 0:64] = dq.astype(jnp.bfloat16)
        if start == starts[-1]:
            dkeys[...] = dk
            dvalues[...] = dv
        else:
            dkeys[0:stop, :] += dk
            dvalues[0:stop, :] += dv
    dpacked_ref[:, 64:128] = dkeys[...].astype(jnp.bfloat16)
    dpacked_ref[:, 128:192] = dvalues[...].astype(jnp.bfloat16)
    dq, dk, dv = back_block(
        extra_ref[...], packed_ref[:, 192:256], packed_ref[:, 256:320],
        xlse_ref[...], xgrad_ref[...], xoutt_ref[...], place_ref[0] * extra_ref.shape[0],
    )
    dextra_ref[...] = dq.astype(jnp.bfloat16)
    dpacked_ref[:, 192:256] = dk.astype(jnp.bfloat16)
    dpacked_ref[:, 256:320] = dv.astype(jnp.bfloat16)


def vmem(count):
    return [pl.BlockSpec(memory_space=pltpu.VMEM)] * count


def attend(place, packed, extra):
    length, rows = packed.shape[0], extra.shape[0]
    bf16, f32 = jnp.bfloat16, jnp.float32
    return pl.pallas_call(
        attend_kernel,
        out_shape=(
            jax.ShapeDtypeStruct((length, HEAD_DIM), bf16),
            jax.ShapeDtypeStruct((HEAD_DIM, length), bf16),
            jax.ShapeDtypeStruct((1, length), f32),
            jax.ShapeDtypeStruct((rows, HEAD_DIM), bf16),
            jax.ShapeDtypeStruct((HEAD_DIM, rows), bf16),
            jax.ShapeDtypeStruct((1, rows), f32),
        ),
        in_specs=[pl.BlockSpec(memory_space=pltpu.SMEM)] + vmem(2),
        out_specs=tuple(vmem(6)),
        compiler_params=pltpu.CompilerParams(vmem_limit_bytes=40 * 2**20),
        name="attend",
    )(place, packed, extra)


def attend_back(place, packed, extra, outt, lse, xoutt, xlse, grad, xgrad):
    length, rows = packed.shape[0], extra.shape[0]
    return pl.pallas_call(
        attend_back_kernel,
        out_shape=(
            jax.ShapeDtypeStruct((length, 5 * HEAD_DIM), jnp.bfloat16),
            jax.ShapeDtypeStruct((rows, HEAD_DIM), jnp.bfloat16),
        ),
        in_specs=[pl.BlockSpec(memory_space=pltpu.SMEM)] + vmem(8),
        out_specs=tuple(vmem(2)),
        scratch_shapes=[
            pltpu.VMEM((length, HEAD_DIM), jnp.float32),
            pltpu.VMEM((length, HEAD_DIM), jnp.float32),
        ],
        compiler_params=pltpu.CompilerParams(vmem_limit_bytes=48 * 2**20),
        name="attend_back",
    )(place, packed, extra, outt, lse, xoutt, xlse, grad, xgrad)


def swap(blocks_of, axis):
    return lax.all_to_all(blocks_of, axis, split_axis=0, concat_axis=0, tiled=True)


def by_head(rows_of, blocks):
    return rows_of[:, : blocks * HEAD_DIM].reshape(-1, blocks, HEAD_DIM).transpose(1, 0, 2)


def from_head(parts, last):
    blocks, rows, _ = parts.shape
    return jnp.concatenate([parts.transpose(1, 0, 2).reshape(rows, blocks * HEAD_DIM), last], axis=1)


def head_attention(query, keys, values):
    blocks = lax.axis_size("ctx")
    rows = query.shape[0]
    place = lax.axis_index("ctx").astype(jnp.int32).reshape(1)
    cut = blocks * HEAD_DIM
    shared = jnp.concatenate([keys[:, cut:], values[:, cut:]], axis=1)
    packed = jnp.concatenate(
        [by_head(query, blocks), by_head(keys, blocks), by_head(values, blocks),
         jnp.broadcast_to(shared[None], (blocks, rows, 2 * HEAD_DIM))],
        axis=2,
    )
    packed = swap(packed, "ctx").reshape(blocks * rows, 5 * HEAD_DIM)
    extra = query[:, cut:]
    out, outt, lse, xout, xoutt, xlse = attend(place, packed, extra)
    back = swap(out.reshape(blocks, rows, HEAD_DIM), "ctx")
    joined = from_head(back, xout)

    def backward(grad_joined):
        grad = swap(by_head(grad_joined, blocks), "ctx").reshape(blocks * rows, HEAD_DIM)
        dpacked, dextra = attend_back(
            place, packed, extra, outt, lse, xoutt, xlse, grad, grad_joined[:, cut:]
        )
        dback = swap(dpacked.reshape(blocks, rows, 5 * HEAD_DIM), "ctx")
        dshared = jnp.sum(dback[:, :, 3 * HEAD_DIM :].astype(jnp.float32), axis=0).astype(jnp.bfloat16)
        return (
            from_head(dback[:, :, :HEAD_DIM], dextra),
            from_head(dback[:, :, HEAD_DIM : 2 * HEAD_DIM], dshared[:, :HEAD_DIM]),
            from_head(dback[:, :, 2 * HEAD_DIM : 3 * HEAD_DIM], dshared[:, HEAD_DIM:]),
        )

    return joined, backward


def ring_attention(query, keys, values):
    position = lax.axis_index("ctx")
    blocks = lax.axis_size("ctx")
    count_rows, width = query.shape
    scale = HEAD_DIM ** (-0.5)
    offsets = jnp.arange(count_rows, dtype=jnp.int32)
    query_pos = position * count_rows + offsets
    shape_heads = (count_rows, HEADS, HEAD_DIM)
    query, keys, values = (part.reshape(shape_heads) for part in (query, keys, values))

    def forward_block(carry, key_block, value_block, source):
        run_max, run_sum, accum = carry
        scores = block_scores(query, key_block, query_pos, source * count_rows + offsets, scale)
        new_max = jnp.maximum(run_max, jnp.max(scores, axis=-1))
        factor = jnp.exp(run_max - new_max)
        weights = jnp.exp(scores - new_max[:, :, None])
        run_sum = run_sum * factor + jnp.sum(weights, axis=-1)
        accum = accum * factor[:, :, None] + jnp.einsum(
            "htk,khe->hte",
            weights.astype(jnp.bfloat16),
            value_block,
            preferred_element_type=jnp.float32,
        )
        return (new_max, run_sum, accum)

    def forward_visit(step, state):
        carry, key_block, value_block, stored = state
        source = (position - step) % blocks
        carry = lax.cond(
            source <= position,
            lambda inner: forward_block(inner, key_block, value_block, source),
            lambda inner: inner,
            carry,
        )
        return (carry, key_block, value_block, stored)

    def forward_step(step, state):
        carry, key_block, value_block, stored = forward_visit(step, state)
        key_block, value_block = shifted((key_block, value_block), "ctx", 1)
        return (carry, key_block, value_block, stored)

    stored_start = ()
    start = (
        jnp.full((HEADS, count_rows), NEG, jnp.float32),
        jnp.zeros((HEADS, count_rows), jnp.float32),
        jnp.zeros((HEADS, count_rows, HEAD_DIM), jnp.float32),
    )
    state = lax.fori_loop(0, blocks - 1, forward_step, (start, keys, values, stored_start))
    (run_max, run_sum, accum), _, _, stored_blocks = forward_visit(blocks - 1, state)
    attended = (accum / run_sum[:, :, None]).transpose(1, 0, 2).astype(jnp.bfloat16)
    lse = run_max + jnp.log(run_sum)

    def backward(grad_joined):
        grad_attended = grad_joined.reshape(shape_heads)
        delta_rows = jnp.sum(
            grad_attended.astype(jnp.float32) * attended.astype(jnp.float32), axis=-1
        ).T

        def backward_block(source, key_block, value_block, grads):
            grad_query, grad_keys, grad_values = grads
            scores = block_scores(query, key_block, query_pos, source * count_rows + offsets, scale)
            prob = jnp.exp(scores - lse[:, :, None])
            grad_values = grad_values + jnp.einsum(
                "htk,the->khe",
                prob.astype(jnp.bfloat16),
                grad_attended,
                preferred_element_type=jnp.float32,
            )
            grad_prob = jnp.einsum(
                "the,khe->htk", grad_attended, value_block, preferred_element_type=jnp.float32
            )
            grad_score = (prob * (grad_prob - delta_rows[:, :, None]) * scale).astype(jnp.bfloat16)
            grad_query = grad_query + jnp.einsum(
                "htk,khe->the", grad_score, key_block, preferred_element_type=jnp.float32
            )
            grad_keys = grad_keys + jnp.einsum(
                "htk,the->khe", grad_score, query, preferred_element_type=jnp.float32
            )
            return (grad_query, grad_keys, grad_values)

        zero_block = jnp.zeros(shape_heads, jnp.float32)

        def backward_step(step, state):
            grad_query, key_block, value_block, grad_keys, grad_values = state
            source = (position - step) % blocks
            grad_query, grad_keys, grad_values = lax.cond(
                source <= position,
                lambda inner: backward_block(source, key_block, value_block, inner),
                lambda inner: inner,
                (grad_query, grad_keys, grad_values),
            )
            key_block, value_block = shifted((key_block, value_block), "ctx", 1)
            grad_keys, grad_values = from_behind((grad_keys, grad_values), "ctx", 1)
            return (grad_query, key_block, value_block, grad_keys, grad_values)

        grad_query, _, _, grad_keys, grad_values = lax.fori_loop(
            0, blocks, backward_step, (zero_block, keys, values, zero_block, zero_block)
        )
        return tuple(
            part.reshape(count_rows, width) for part in (grad_query, grad_keys, grad_values)
        )

    return attended.reshape(count_rows, width), backward


def other_half(value):
    return lax.ppermute(value, "fsdp", [(0, 1), (1, 0)])


def partner(value, bit):
    count = lax.axis_size("ctx")
    return lax.ppermute(value, "ctx", [(source, source ^ bit) for source in range(count)])


def after(value, earlier):
    return lax.optimization_barrier((value, earlier))[0]


def gather_weights(shards):
    quarter = lax.axis_index("ctx") % 4
    place = lax.axis_index("fsdp")
    wholes, earlier = [], None
    for shard in shards:
        depth, columns = shard.shape
        parts = shard.reshape(4, depth // 4, columns)
        piece = lax.dynamic_slice_in_dim(parts, quarter, 1, 0)
        if earlier is not None:
            piece = after(piece, earlier)
        first = other_half(piece)
        earlier = first
        second = partner(first, 2)
        third = partner(first, 1)
        fourth = partner(second, 1)
        whole = jnp.concatenate([parts, parts], axis=0)
        base = (1 - place) * 4
        for got, bits in ((first, 0), (second, 2), (third, 1), (fourth, 3)):
            whole = lax.dynamic_update_slice_in_dim(whole, got, base + (quarter ^ bits), 0)
        wholes.append(whole.reshape(2 * depth, columns))
    return wholes


def on_device(
    block_input,
    cotangent,
    first_gain,
    first_shift,
    qkv_weight,
    query_bias,
    value_bias,
    out_weight,
    out_bias,
    second_gain,
    second_shift,
    up_weight,
    up_bias,
    down_weight,
    down_bias,
):
    fsdp = lax.axis_size("fsdp")
    blocks = lax.axis_size("ctx")
    place = lax.axis_index("fsdp")
    width = HEADS * HEAD_DIM
    f32, bf16 = jnp.float32, jnp.bfloat16
    small = (
        first_gain, first_shift, query_bias, value_bias, out_bias, second_gain, second_shift,
        down_bias, up_bias,
    )
    sizes = [part.shape[0] for part in small]
    gathered = lax.all_gather(jnp.concatenate(small), "fsdp", axis=0, tiled=False)
    whole_small, at = [], 0
    for size in sizes:
        whole_small.append(gathered[:, at : at + size].reshape(fsdp * size).astype(f32))
        at += size
    gain_one, shift_one, bias_q, bias_v, bias_o, gain_two, shift_two, bias_d, bias_u = whole_small
    shards = (qkv_weight, out_weight, up_weight, down_weight)
    paired = fsdp == 2 and blocks % 4 == 0
    if paired:
        whole_qkv, whole_out, whole_up, whole_down = gather_weights(shards)
    else:
        whole_qkv, whole_out, whole_up, whole_down = (
            lax.all_gather(part, "fsdp", axis=0, tiled=True) for part in shards
        )
    rows = block_input.astype(f32)
    first_norm, first_hat, first_rstd = normalize(rows, gain_one, shift_one)
    first_act = first_norm.astype(bf16)
    qkv = jnp.dot(first_act, whole_qkv, preferred_element_type=f32)
    query = (qkv[:, :width] + bias_q).astype(bf16)
    keys = qkv[:, width : 2 * width].astype(bf16)
    values = (qkv[:, 2 * width :] + bias_v).astype(bf16)
    attention = head_attention if HEADS == blocks + 1 else ring_attention
    joined, attention_back = attention(query, keys, values)
    mid = rows + jnp.dot(joined, whole_out, preferred_element_type=f32) + bias_o
    second_norm, second_hat, second_rstd = normalize(mid, gain_two, shift_two)
    second_act = second_norm.astype(bf16)
    pre = jnp.dot(second_act, whole_up, preferred_element_type=f32) + bias_u
    act = gelu_tanh(pre).astype(bf16)
    block_output = mid + jnp.dot(act, whole_down, preferred_element_type=f32) + bias_d

    def left(part):
        if paired:
            half = part.shape[1] // 2
            own = lax.dynamic_slice_in_dim(part, place * half, half, 1)
            sent = lax.dynamic_slice_in_dim(part, (1 - place) * half, half, 1)
            return jnp.concatenate([own, other_half(sent)], axis=0)
        return lax.all_to_all(part, "fsdp", split_axis=1, concat_axis=0, tiled=True)

    def right(part):
        if paired:
            return jnp.concatenate([part, other_half(part)], axis=0)
        return lax.all_gather(part, "fsdp", axis=0, tiled=True)

    def weight_grad(left_part, right_part):
        return contract(left(left_part), right(right_part), 0, 0).astype(bf16)

    def total(value, earlier=None):
        if earlier is not None:
            value = after(value, earlier)
        return lax.psum(value, "ctx")

    cot_float = cotangent.astype(f32)
    grad_down = total(weight_grad(act, cotangent))
    grad_down_bias = jnp.sum(cot_float, axis=0)
    grad_pre = gelu_back(pre, contract(cotangent, whole_down, 1, 1))
    grad_pre_b = grad_pre.astype(bf16)
    grad_up = total(weight_grad(second_act, grad_pre_b), grad_down)
    grad_up_bias = jnp.sum(grad_pre, axis=0)
    grad_second = contract(grad_pre_b, whole_up, 1, 1)
    grad_second_gain = jnp.sum(grad_second * second_hat, axis=0)
    grad_second_shift = jnp.sum(grad_second, axis=0)
    grad_mid = cot_float + normalize_back(grad_second, second_hat, second_rstd, gain_two)
    grad_mid_b = grad_mid.astype(bf16)
    grad_out = total(weight_grad(joined, grad_mid_b), grad_up)
    grad_out_bias = jnp.sum(grad_mid, axis=0)
    grad_attended = contract(grad_mid_b, whole_out, 1, 1).astype(bf16)
    grad_query, grad_keys, grad_values = attention_back(grad_attended)
    grad_query_bias = jnp.sum(grad_query.astype(f32), axis=0)
    grad_value_bias = jnp.sum(grad_values.astype(f32), axis=0)
    grad_qkv_b = jnp.concatenate([grad_query, grad_keys, grad_values], axis=1).astype(bf16)
    grad_qkv = weight_grad(first_act, grad_qkv_b)
    grad_first = contract(grad_qkv_b, whole_qkv, 1, 1)
    grad_first_gain = jnp.sum(grad_first * first_hat, axis=0)
    grad_first_shift = jnp.sum(grad_first, axis=0)
    input_grad = grad_mid + normalize_back(grad_first, first_hat, first_rstd, gain_one)
    vectors = (
        grad_first_gain, grad_first_shift, grad_query_bias, grad_value_bias, grad_out_bias,
        grad_second_gain, grad_second_shift, grad_down_bias, grad_up_bias,
    )
    packed_vectors = jnp.concatenate([part.reshape(fsdp, -1) for part in vectors], axis=1)
    mine = lax.dynamic_index_in_dim(packed_vectors, place, 0, keepdims=False)
    if paired:
        sent = lax.dynamic_index_in_dim(packed_vectors, 1 - place, 0, keepdims=False)
        mine = mine + other_half(sent)
    else:
        mine = lax.psum_scatter(packed_vectors, "fsdp", scatter_dimension=0, tiled=True)[0]
    grad_qkv, mine = total((grad_qkv, mine.astype(bf16)), grad_out)
    mine = mine.astype(f32)
    shards, at = [], 0
    for size in sizes:
        shards.append(mine[at : at + size])
        at += size
    gain_g1, shift_g1, bias_gq, bias_gv, bias_go, gain_g2, shift_g2, bias_gd, bias_gu = shards
    return (
        block_output,
        input_grad,
        gain_g1,
        shift_g1,
        grad_qkv.astype(f32),
        bias_gq,
        bias_gv,
        grad_out.astype(f32),
        bias_go,
        gain_g2,
        shift_g2,
        grad_up.astype(f32),
        bias_gu,
        grad_down.astype(f32),
        bias_gd,
    )


def solution(mesh):
    placed = (
        P(("fsdp", "ctx"), None),
        P(("fsdp", "ctx"), None),
        P("fsdp"),
        P("fsdp"),
        P("fsdp", None),
        P("fsdp"),
        P("fsdp"),
        P("fsdp", None),
        P("fsdp"),
        P("fsdp"),
        P("fsdp"),
        P("fsdp", None),
        P("fsdp"),
        P("fsdp", None),
        P("fsdp"),
    )
    return jax.shard_map(
        on_device,
        mesh=mesh,
        in_specs=placed,
        out_specs=(
            P(("fsdp", "ctx"), None),
            P(("fsdp", "ctx"), None),
            P("fsdp"),
            P("fsdp"),
            P("fsdp", None),
            P("fsdp"),
            P("fsdp"),
            P("fsdp", None),
            P("fsdp"),
            P("fsdp"),
            P("fsdp"),
            P("fsdp", None),
            P("fsdp"),
            P("fsdp", None),
            P("fsdp"),
        ),
        check_vma=False,
    )
```

```python
import functools

import jax
import jax.numpy as jnp
from jax import lax
from jax.experimental import pallas as pl
from jax.experimental.pallas import tpu as pltpu
from jax.sharding import PartitionSpec as P

HEADS = 17
HEAD_DIM = 64


EPS = 1e-05
NEG = -1e30


def shifted(block, axis, distance):
    devices = range(lax.axis_size(axis))
    route = [(i - distance, i) for i in devices if i - distance in devices]
    return lax.ppermute(block, axis, route)


def from_behind(value, axis, steps):
    count = lax.axis_size(axis)
    pairs = [(source, (source + steps) % count) for source in range(count)]
    return lax.ppermute(value, axis, pairs)


def normalize(rows, gain, shift):
    mean = jnp.mean(rows, axis=-1, keepdims=True)
    centered = rows - mean
    rstd = lax.rsqrt(jnp.mean(centered * centered, axis=-1, keepdims=True) + EPS)
    hat = centered * rstd
    return (hat * gain + shift, hat, rstd)


def normalize_back(grad, hat, rstd, gain):
    scaled = grad * gain
    return rstd * (
        scaled
        - jnp.mean(scaled, axis=-1, keepdims=True)
        - hat * jnp.mean(scaled * hat, axis=-1, keepdims=True)
    )


def gelu_tanh(value):
    return jax.nn.gelu(value, approximate=True)


def gelu_back(pre, grad):
    _, pull = jax.vjp(gelu_tanh, pre)
    return pull(grad)[0]


def contract(left, right, left_dim, right_dim):
    return lax.dot_general(
        left, right, (((left_dim,), (right_dim,)), ((), ())), preferred_element_type=jnp.float32
    )


def block_scores(query, key_block, query_pos, key_pos, scale):
    scores = (
        jnp.einsum("the,khe->htk", query, key_block, preferred_element_type=jnp.float32) * scale
    )
    allowed = key_pos[None, None, :] <= query_pos[None, :, None]
    return jnp.where(allowed, scores, NEG)


def matmul(left, right, left_dim, right_dim):
    return lax.dot_general(
        left, right, (((left_dim,), (right_dim,)), ((), ())), preferred_element_type=jnp.float32
    )


QUERY_ROWS = 256


def softmax_block(query, keys, values, first_query):
    scores = matmul(keys, query, 1, 1)
    key_pos = lax.broadcasted_iota(jnp.int32, scores.shape, 0)
    query_pos = lax.broadcasted_iota(jnp.int32, scores.shape, 1) + first_query
    scores = jnp.where(key_pos <= query_pos, scores, NEG)
    top = jnp.max(scores, axis=0, keepdims=True)
    weights = jnp.exp(scores - top)
    total = jnp.sum(weights, axis=0, keepdims=True)
    mixed = matmul(values, weights.astype(jnp.bfloat16), 0, 0) / total
    return mixed.astype(jnp.bfloat16), top + jnp.log(total)


def attend_kernel(place_ref, packed_ref, extra_ref, out_ref, outt_ref, lse_ref, xout_ref, xoutt_ref, xlse_ref):
    length = packed_ref.shape[0]
    scale = HEAD_DIM ** (-0.5)
    for start in range(0, length, QUERY_ROWS):
        stop = start + QUERY_ROWS
        query = packed_ref[start:stop, 0:64] * scale
        mixed, lse = softmax_block(
            query.astype(jnp.bfloat16), packed_ref[0:stop, 64:128], packed_ref[0:stop, 128:192], start
        )
        outt_ref[:, start:stop] = mixed
        out_ref[start:stop, :] = mixed.astype(jnp.float32).T.astype(jnp.bfloat16)
        lse_ref[:, start:stop] = lse
    query = (extra_ref[...] * scale).astype(jnp.bfloat16)
    mixed, lse = softmax_block(
        query, packed_ref[:, 192:256], packed_ref[:, 256:320], place_ref[0] * extra_ref.shape[0]
    )
    xoutt_ref[...] = mixed
    xout_ref[...] = mixed.astype(jnp.float32).T.astype(jnp.bfloat16)
    xlse_ref[...] = lse


def back_block(query, keys, values, lse, grad, mixed, first_query):
    scale = HEAD_DIM ** (-0.5)
    query = (query * scale).astype(jnp.bfloat16)
    scores = matmul(keys, query, 1, 1)
    key_pos = lax.broadcasted_iota(jnp.int32, scores.shape, 0)
    query_pos = lax.broadcasted_iota(jnp.int32, scores.shape, 1) + first_query
    prob = jnp.where(key_pos <= query_pos, jnp.exp(scores - lse), 0.0)
    grad_values = matmul(prob.astype(jnp.bfloat16), grad, 1, 0)
    grad_prob = matmul(values, grad, 1, 1)
    delta = jnp.sum(
        grad.astype(jnp.float32).T * mixed.astype(jnp.float32), axis=0, keepdims=True
    )
    grad_score = (prob * (grad_prob - delta)).astype(jnp.bfloat16)
    grad_keys = matmul(grad_score, query, 1, 0)
    grad_query = matmul(keys, grad_score, 0, 0) * scale
    return grad_query.T, grad_keys, grad_values


def attend_back_kernel(
    place_ref, packed_ref, extra_ref, outt_ref, lse_ref, xoutt_ref, xlse_ref, grad_ref, xgrad_ref,
    dpacked_ref, dextra_ref, dkeys, dvalues,
):
    length = packed_ref.shape[0]
    starts = list(range(0, length, QUERY_ROWS))
    for start in reversed(starts):
        stop = start + QUERY_ROWS
        dq, dk, dv = back_block(
            packed_ref[start:stop, 0:64], packed_ref[0:stop, 64:128], packed_ref[0:stop, 128:192],
            lse_ref[:, start:stop], grad_ref[start:stop, :], outt_ref[:, start:stop], start,
        )
        dpacked_ref[start:stop, 0:64] = dq.astype(jnp.bfloat16)
        if start == starts[-1]:
            dkeys[...] = dk
            dvalues[...] = dv
        else:
            dkeys[0:stop, :] += dk
            dvalues[0:stop, :] += dv
    dpacked_ref[:, 64:128] = dkeys[...].astype(jnp.bfloat16)
    dpacked_ref[:, 128:192] = dvalues[...].astype(jnp.bfloat16)
    dq, dk, dv = back_block(
        extra_ref[...], packed_ref[:, 192:256], packed_ref[:, 256:320],
        xlse_ref[...], xgrad_ref[...], xoutt_ref[...], place_ref[0] * extra_ref.shape[0],
    )
    dextra_ref[...] = dq.astype(jnp.bfloat16)
    dpacked_ref[:, 192:256] = dk.astype(jnp.bfloat16)
    dpacked_ref[:, 256:320] = dv.astype(jnp.bfloat16)


def vmem(count):
    return [pl.BlockSpec(memory_space=pltpu.VMEM)] * count


def attend(place, packed, extra):
    length, rows = packed.shape[0], extra.shape[0]
    bf16, f32 = jnp.bfloat16, jnp.float32
    return pl.pallas_call(
        attend_kernel,
        out_shape=(
            jax.ShapeDtypeStruct((length, HEAD_DIM), bf16),
            jax.ShapeDtypeStruct((HEAD_DIM, length), bf16),
            jax.ShapeDtypeStruct((1, length), f32),
            jax.ShapeDtypeStruct((rows, HEAD_DIM), bf16),
            jax.ShapeDtypeStruct((HEAD_DIM, rows), bf16),
            jax.ShapeDtypeStruct((1, rows), f32),
        ),
        in_specs=[pl.BlockSpec(memory_space=pltpu.SMEM)] + vmem(2),
        out_specs=tuple(vmem(6)),
        compiler_params=pltpu.CompilerParams(vmem_limit_bytes=40 * 2**20),
        name="attend",
    )(place, packed, extra)


def attend_back(place, packed, extra, outt, lse, xoutt, xlse, grad, xgrad):
    length, rows = packed.shape[0], extra.shape[0]
    return pl.pallas_call(
        attend_back_kernel,
        out_shape=(
            jax.ShapeDtypeStruct((length, 5 * HEAD_DIM), jnp.bfloat16),
            jax.ShapeDtypeStruct((rows, HEAD_DIM), jnp.bfloat16),
        ),
        in_specs=[pl.BlockSpec(memory_space=pltpu.SMEM)] + vmem(8),
        out_specs=tuple(vmem(2)),
        scratch_shapes=[
            pltpu.VMEM((length, HEAD_DIM), jnp.float32),
            pltpu.VMEM((length, HEAD_DIM), jnp.float32),
        ],
        compiler_params=pltpu.CompilerParams(vmem_limit_bytes=48 * 2**20),
        name="attend_back",
    )(place, packed, extra, outt, lse, xoutt, xlse, grad, xgrad)


def swap(blocks_of, axis):
    return lax.all_to_all(blocks_of, axis, split_axis=0, concat_axis=0, tiled=True)


def by_head(rows_of, blocks):
    return rows_of[:, : blocks * HEAD_DIM].reshape(-1, blocks, HEAD_DIM).transpose(1, 0, 2)


def from_head(parts, last):
    blocks, rows, _ = parts.shape
    return jnp.concatenate([parts.transpose(1, 0, 2).reshape(rows, blocks * HEAD_DIM), last], axis=1)


def head_attention(query, keys, values):
    blocks = lax.axis_size("ctx")
    rows = query.shape[0]
    place = lax.axis_index("ctx").astype(jnp.int32).reshape(1)
    cut = blocks * HEAD_DIM
    shared = jnp.concatenate([keys[:, cut:], values[:, cut:]], axis=1)
    packed = jnp.concatenate(
        [by_head(query, blocks), by_head(keys, blocks), by_head(values, blocks),
         jnp.broadcast_to(shared[None], (blocks, rows, 2 * HEAD_DIM))],
        axis=2,
    )
    packed = swap(packed, "ctx").reshape(blocks * rows, 5 * HEAD_DIM)
    extra = query[:, cut:]
    out, outt, lse, xout, xoutt, xlse = attend(place, packed, extra)
    back = swap(out.reshape(blocks, rows, HEAD_DIM), "ctx")
    joined = from_head(back, xout)

    def backward(grad_joined):
        grad = swap(by_head(grad_joined, blocks), "ctx").reshape(blocks * rows, HEAD_DIM)
        dpacked, dextra = attend_back(
            place, packed, extra, outt, lse, xoutt, xlse, grad, grad_joined[:, cut:]
        )
        dback = swap(dpacked.reshape(blocks, rows, 5 * HEAD_DIM), "ctx")
        dshared = jnp.sum(dback[:, :, 3 * HEAD_DIM :].astype(jnp.float32), axis=0).astype(jnp.bfloat16)
        return (
            from_head(dback[:, :, :HEAD_DIM], dextra),
            from_head(dback[:, :, HEAD_DIM : 2 * HEAD_DIM], dshared[:, :HEAD_DIM]),
            from_head(dback[:, :, 2 * HEAD_DIM : 3 * HEAD_DIM], dshared[:, HEAD_DIM:]),
        )

    return joined, backward


def ring_attention(query, keys, values):
    position = lax.axis_index("ctx")
    blocks = lax.axis_size("ctx")
    count_rows, width = query.shape
    scale = HEAD_DIM ** (-0.5)
    offsets = jnp.arange(count_rows, dtype=jnp.int32)
    query_pos = position * count_rows + offsets
    shape_heads = (count_rows, HEADS, HEAD_DIM)
    query, keys, values = (part.reshape(shape_heads) for part in (query, keys, values))

    def forward_block(carry, key_block, value_block, source):
        run_max, run_sum, accum = carry
        scores = block_scores(query, key_block, query_pos, source * count_rows + offsets, scale)
        new_max = jnp.maximum(run_max, jnp.max(scores, axis=-1))
        factor = jnp.exp(run_max - new_max)
        weights = jnp.exp(scores - new_max[:, :, None])
        run_sum = run_sum * factor + jnp.sum(weights, axis=-1)
        accum = accum * factor[:, :, None] + jnp.einsum(
            "htk,khe->hte",
            weights.astype(jnp.bfloat16),
            value_block,
            preferred_element_type=jnp.float32,
        )
        return (new_max, run_sum, accum)

    def forward_visit(step, state):
        carry, key_block, value_block, stored = state
        source = (position - step) % blocks
        carry = lax.cond(
            source <= position,
            lambda inner: forward_block(inner, key_block, value_block, source),
            lambda inner: inner,
            carry,
        )
        return (carry, key_block, value_block, stored)

    def forward_step(step, state):
        carry, key_block, value_block, stored = forward_visit(step, state)
        key_block, value_block = shifted((key_block, value_block), "ctx", 1)
        return (carry, key_block, value_block, stored)

    stored_start = ()
    start = (
        jnp.full((HEADS, count_rows), NEG, jnp.float32),
        jnp.zeros((HEADS, count_rows), jnp.float32),
        jnp.zeros((HEADS, count_rows, HEAD_DIM), jnp.float32),
    )
    state = lax.fori_loop(0, blocks - 1, forward_step, (start, keys, values, stored_start))
    (run_max, run_sum, accum), _, _, stored_blocks = forward_visit(blocks - 1, state)
    attended = (accum / run_sum[:, :, None]).transpose(1, 0, 2).astype(jnp.bfloat16)
    lse = run_max + jnp.log(run_sum)

    def backward(grad_joined):
        grad_attended = grad_joined.reshape(shape_heads)
        delta_rows = jnp.sum(
            grad_attended.astype(jnp.float32) * attended.astype(jnp.float32), axis=-1
        ).T

        def backward_block(source, key_block, value_block, grads):
            grad_query, grad_keys, grad_values = grads
            scores = block_scores(query, key_block, query_pos, source * count_rows + offsets, scale)
            prob = jnp.exp(scores - lse[:, :, None])
            grad_values = grad_values + jnp.einsum(
                "htk,the->khe",
                prob.astype(jnp.bfloat16),
                grad_attended,
                preferred_element_type=jnp.float32,
            )
            grad_prob = jnp.einsum(
                "the,khe->htk", grad_attended, value_block, preferred_element_type=jnp.float32
            )
            grad_score = (prob * (grad_prob - delta_rows[:, :, None]) * scale).astype(jnp.bfloat16)
            grad_query = grad_query + jnp.einsum(
                "htk,khe->the", grad_score, key_block, preferred_element_type=jnp.float32
            )
            grad_keys = grad_keys + jnp.einsum(
                "htk,the->khe", grad_score, query, preferred_element_type=jnp.float32
            )
            return (grad_query, grad_keys, grad_values)

        zero_block = jnp.zeros(shape_heads, jnp.float32)

        def backward_step(step, state):
            grad_query, key_block, value_block, grad_keys, grad_values = state
            source = (position - step) % blocks
            grad_query, grad_keys, grad_values = lax.cond(
                source <= position,
                lambda inner: backward_block(source, key_block, value_block, inner),
                lambda inner: inner,
                (grad_query, grad_keys, grad_values),
            )
            key_block, value_block = shifted((key_block, value_block), "ctx", 1)
            grad_keys, grad_values = from_behind((grad_keys, grad_values), "ctx", 1)
            return (grad_query, key_block, value_block, grad_keys, grad_values)

        grad_query, _, _, grad_keys, grad_values = lax.fori_loop(
            0, blocks, backward_step, (zero_block, keys, values, zero_block, zero_block)
        )
        return tuple(
            part.reshape(count_rows, width) for part in (grad_query, grad_keys, grad_values)
        )

    return attended.reshape(count_rows, width), backward


def other_half(value):
    return lax.ppermute(value, "fsdp", [(0, 1), (1, 0)])


def spans(columns, pieces):
    tiles = -(-columns // 128)
    step = -(-tiles // pieces) * 128
    return [(at, min(step, columns - at)) for at in range(0, columns, step)]


def gather_kernel(plan, *refs):
    count = len(plan)
    shards, wholes = refs[:count], refs[count : 2 * count]
    own_sem, send_sem, recv_sem = refs[2 * count :]
    place, spot = lax.axis_index("fsdp"), lax.axis_index("ctx")
    quarter = lax.rem(spot, 4)
    across = (1 - place, spot)
    beside_core = spot + 1 - 2 * lax.rem(spot, 2)
    beside_chip = spot + 2 - 4 * (quarter // 2)
    core, chip = (place, beside_core), (place, beside_chip)
    twin = lax.rem(beside_chip, 4)
    barrier = pltpu.get_barrier_semaphore()
    for device in (across, core, chip):
        pl.semaphore_signal(barrier, inc=1, device_id=device, device_id_type=pl.DeviceIdType.MESH)
    pl.semaphore_wait(barrier, 3)
    mine, theirs = place * 4, (1 - place) * 4
    parts = [(which, span) for which in range(count) for span in plan[which]]

    def send(part, kind, source, slot, device):
        which, (at, size) = parts[part]
        return pltpu.make_async_remote_copy(
            src_ref=source,
            dst_ref=wholes[which].at[slot, :, at : at + size],
            send_sem=send_sem.at[part, kind],
            recv_sem=recv_sem.at[part, kind],
            device_id=device,
            device_id_type=pl.DeviceIdType.MESH,
        )

    def held(part, slot):
        which, (at, size) = parts[part]
        return wholes[which].at[slot, :, at : at + size]

    fetch, over_chip, over_core, again = [], [], [], []
    for part, (which, (at, size)) in enumerate(parts):
        source = shards[which].at[quarter, :, at : at + size]
        fetch.append(send(part, 0, source, mine + quarter, across))
        over_chip.append(send(part, 1, held(part, theirs + quarter), theirs + quarter, chip))
        over_core.append(send(part, 2, held(part, theirs + quarter), theirs + quarter, core))
        again.append(send(part, 3, held(part, theirs + twin), theirs + twin, core))
        fetch[part].start()
    locals_ = []
    for which in range(count):
        copy = pltpu.make_async_copy(
            shards[which], wholes[which].at[pl.ds(mine, 4)], own_sem.at[which]
        )
        copy.start()
        locals_.append(copy)
    total = len(parts)
    for part in range(total + 1):
        if part < total:
            fetch[part].wait_recv()
            over_chip[part].start()
            over_core[part].start()
        if part > 0:
            over_chip[part - 1].wait_recv()
            again[part - 1].start()
    for part in range(total):
        over_core[part].wait_recv()
        again[part].wait_recv()
        for copy in (fetch, over_chip, over_core, again):
            copy[part].wait_send()
    for copy in locals_:
        copy.wait()


def gather_weights(shards, pieces, identity):
    quarters = [shard.reshape(4, shard.shape[0] // 4, shard.shape[1]) for shard in shards]
    plan = [spans(shard.shape[1], piece) for shard, piece in zip(shards, pieces)]
    total = sum(len(part) for part in plan)
    size = sum(shard.size for shard in shards)
    wholes = pl.pallas_call(
        functools.partial(gather_kernel, plan),
        out_shape=tuple(
            jax.ShapeDtypeStruct((8,) + part.shape[1:], part.dtype) for part in quarters
        ),
        in_specs=[pl.BlockSpec(memory_space=pl.ANY)] * len(shards),
        out_specs=tuple([pl.BlockSpec(memory_space=pl.ANY)] * len(shards)),
        scratch_shapes=[
            pltpu.SemaphoreType.DMA((len(shards),)),
            pltpu.SemaphoreType.DMA((total, 4)),
            pltpu.SemaphoreType.DMA((total, 4)),
        ],
        compiler_params=pltpu.CompilerParams(collective_id=identity, has_side_effects=True),
        cost_estimate=pl.CostEstimate(flops=0, bytes_accessed=16 * size, transcendentals=0),
        name="gather_weights",
    )(*quarters)
    return [
        whole.reshape(2 * shard.shape[0], shard.shape[1]) for whole, shard in zip(wholes, shards)
    ]


def on_device(
    block_input,
    cotangent,
    first_gain,
    first_shift,
    qkv_weight,
    query_bias,
    value_bias,
    out_weight,
    out_bias,
    second_gain,
    second_shift,
    up_weight,
    up_bias,
    down_weight,
    down_bias,
):
    fsdp = lax.axis_size("fsdp")
    blocks = lax.axis_size("ctx")
    place = lax.axis_index("fsdp")
    width = HEADS * HEAD_DIM
    f32, bf16 = jnp.float32, jnp.bfloat16
    small = (
        first_gain, first_shift, query_bias, value_bias, out_bias, second_gain, second_shift,
        down_bias, up_bias,
    )
    sizes = [part.shape[0] for part in small]
    paired = fsdp == 2 and blocks % 4 == 0
    packed_small = jnp.concatenate(small)
    if paired:
        apart = other_half(packed_small)
        gathered = jnp.where(
            place == 0, jnp.stack([packed_small, apart]), jnp.stack([apart, packed_small])
        )
    else:
        gathered = lax.all_gather(packed_small, "fsdp", axis=0, tiled=False)
    whole_small, at = [], 0
    for size in sizes:
        whole_small.append(gathered[:, at : at + size].reshape(fsdp * size).astype(f32))
        at += size
    gain_one, shift_one, bias_q, bias_v, bias_o, gain_two, shift_two, bias_d, bias_u = whole_small
    if paired:
        (whole_qkv,) = gather_weights((qkv_weight,), (4,), 1)
    else:
        whole_qkv = lax.all_gather(qkv_weight, "fsdp", axis=0, tiled=True)
    rows = block_input.astype(f32)
    first_norm, first_hat, first_rstd = normalize(rows, gain_one, shift_one)
    first_act = first_norm.astype(bf16)
    qkv = jnp.dot(first_act, whole_qkv, preferred_element_type=f32)
    query = (qkv[:, :width] + bias_q).astype(bf16)
    keys = qkv[:, width : 2 * width].astype(bf16)
    values = (qkv[:, 2 * width :] + bias_v).astype(bf16)
    later = (out_weight, up_weight, down_weight)
    if paired:
        later = lax.optimization_barrier((later, qkv))[0]
        whole_out, whole_up, whole_down = gather_weights(later, (1, 3, 3), 2)
    else:
        whole_out, whole_up, whole_down = (
            lax.all_gather(part, "fsdp", axis=0, tiled=True) for part in later
        )
    attention = head_attention if HEADS == blocks + 1 else ring_attention
    joined, attention_back = attention(query, keys, values)
    mid = rows + jnp.dot(joined, whole_out, preferred_element_type=f32) + bias_o
    second_norm, second_hat, second_rstd = normalize(mid, gain_two, shift_two)
    second_act = second_norm.astype(bf16)
    pre = jnp.dot(second_act, whole_up, preferred_element_type=f32) + bias_u
    act = gelu_tanh(pre).astype(bf16)
    block_output = mid + jnp.dot(act, whole_down, preferred_element_type=f32) + bias_d

    def left(part):
        if paired:
            half = part.shape[1] // 2
            own = lax.dynamic_slice_in_dim(part, place * half, half, 1)
            sent = lax.dynamic_slice_in_dim(part, (1 - place) * half, half, 1)
            return jnp.concatenate([own, other_half(sent)], axis=0)
        return lax.all_to_all(part, "fsdp", split_axis=1, concat_axis=0, tiled=True)

    def right(part):
        if paired:
            return jnp.concatenate([part, other_half(part)], axis=0)
        return lax.all_gather(part, "fsdp", axis=0, tiled=True)

    def weight_grad(left_part, right_part):
        return contract(left(left_part), right(right_part), 0, 0).astype(bf16)

    cot_float = cotangent.astype(f32)
    grad_down = weight_grad(act, cotangent)
    grad_down_bias = jnp.sum(cot_float, axis=0)
    grad_pre = gelu_back(pre, contract(cotangent, whole_down, 1, 1))
    grad_pre_b = grad_pre.astype(bf16)
    grad_up = weight_grad(second_act, grad_pre_b)
    grad_up_bias = jnp.sum(grad_pre, axis=0)
    grad_second = contract(grad_pre_b, whole_up, 1, 1)
    grad_second_gain = jnp.sum(grad_second * second_hat, axis=0)
    grad_second_shift = jnp.sum(grad_second, axis=0)
    grad_mid = cot_float + normalize_back(grad_second, second_hat, second_rstd, gain_two)
    grad_mid_b = grad_mid.astype(bf16)
    grad_out = weight_grad(joined, grad_mid_b)
    grad_out_bias = jnp.sum(grad_mid, axis=0)
    grad_attended = contract(grad_mid_b, whole_out, 1, 1).astype(bf16)
    grad_query, grad_keys, grad_values = attention_back(grad_attended)
    grad_query_bias = jnp.sum(grad_query.astype(f32), axis=0)
    grad_value_bias = jnp.sum(grad_values.astype(f32), axis=0)
    grad_qkv_b = jnp.concatenate([grad_query, grad_keys, grad_values], axis=1).astype(bf16)
    grad_qkv = weight_grad(first_act, grad_qkv_b)
    grad_first = contract(grad_qkv_b, whole_qkv, 1, 1)
    grad_first_gain = jnp.sum(grad_first * first_hat, axis=0)
    grad_first_shift = jnp.sum(grad_first, axis=0)
    input_grad = grad_mid + normalize_back(grad_first, first_hat, first_rstd, gain_one)
    vectors = (
        grad_first_gain, grad_first_shift, grad_query_bias, grad_value_bias, grad_out_bias,
        grad_second_gain, grad_second_shift, grad_down_bias, grad_up_bias,
    )
    packed_vectors = jnp.concatenate([part.reshape(fsdp, -1) for part in vectors], axis=1)
    mine = lax.dynamic_index_in_dim(packed_vectors, place, 0, keepdims=False)
    if paired:
        sent = lax.dynamic_index_in_dim(packed_vectors, 1 - place, 0, keepdims=False)
        mine = mine + other_half(sent)
    else:
        mine = lax.psum_scatter(packed_vectors, "fsdp", scatter_dimension=0, tiled=True)[0]
    depth, columns = grad_qkv.shape
    spare = -(-mine.shape[0] // (8 * columns)) * 8
    below = jnp.pad(mine.astype(bf16), (0, spare * columns - mine.shape[0]))
    grad_qkv = jnp.concatenate([grad_qkv, below.reshape(spare, columns)], axis=0)
    grad_qkv, grad_out, grad_up, grad_down = lax.psum(
        (grad_qkv, grad_out, grad_up, grad_down), "ctx"
    )
    mine = grad_qkv[depth:].reshape(-1).astype(f32)
    grad_qkv = grad_qkv[:depth]
    shards, at = [], 0
    for size in sizes:
        shards.append(mine[at : at + size])
        at += size
    gain_g1, shift_g1, bias_gq, bias_gv, bias_go, gain_g2, shift_g2, bias_gd, bias_gu = shards
    return (
        block_output,
        input_grad,
        gain_g1,
        shift_g1,
        grad_qkv.astype(f32),
        bias_gq,
        bias_gv,
        grad_out.astype(f32),
        bias_go,
        gain_g2,
        shift_g2,
        grad_up.astype(f32),
        bias_gu,
        grad_down.astype(f32),
        bias_gd,
    )


def solution(mesh):
    placed = (
        P(("fsdp", "ctx"), None),
        P(("fsdp", "ctx"), None),
        P("fsdp"),
        P("fsdp"),
        P("fsdp", None),
        P("fsdp"),
        P("fsdp"),
        P("fsdp", None),
        P("fsdp"),
        P("fsdp"),
        P("fsdp"),
        P("fsdp", None),
        P("fsdp"),
        P("fsdp", None),
        P("fsdp"),
    )
    return jax.shard_map(
        on_device,
        mesh=mesh,
        in_specs=placed,
        out_specs=(
            P(("fsdp", "ctx"), None),
            P(("fsdp", "ctx"), None),
            P("fsdp"),
            P("fsdp"),
            P("fsdp", None),
            P("fsdp"),
            P("fsdp"),
            P("fsdp", None),
            P("fsdp"),
            P("fsdp"),
            P("fsdp"),
            P("fsdp", None),
            P("fsdp"),
            P("fsdp", None),
            P("fsdp"),
        ),
        check_vma=False,
    )
```

```python
import jax
import jax.numpy as jnp
from jax import lax
from jax.experimental import pallas as pl
from jax.experimental.pallas import tpu as pltpu
from jax.sharding import PartitionSpec as P

HEADS = 17
HEAD_DIM = 64


EPS = 1e-05
NEG = -1e30


def shifted(block, axis, distance):
    devices = range(lax.axis_size(axis))
    route = [(i - distance, i) for i in devices if i - distance in devices]
    return lax.ppermute(block, axis, route)


def from_behind(value, axis, steps):
    count = lax.axis_size(axis)
    pairs = [(source, (source + steps) % count) for source in range(count)]
    return lax.ppermute(value, axis, pairs)


def normalize(rows, gain, shift):
    mean = jnp.mean(rows, axis=-1, keepdims=True)
    centered = rows - mean
    rstd = lax.rsqrt(jnp.mean(centered * centered, axis=-1, keepdims=True) + EPS)
    hat = centered * rstd
    return (hat * gain + shift, hat, rstd)


def normalize_back(grad, hat, rstd, gain):
    scaled = grad * gain
    return rstd * (
        scaled
        - jnp.mean(scaled, axis=-1, keepdims=True)
        - hat * jnp.mean(scaled * hat, axis=-1, keepdims=True)
    )


def gelu_tanh(value):
    return jax.nn.gelu(value, approximate=True)


def gelu_back(pre, grad):
    _, pull = jax.vjp(gelu_tanh, pre)
    return pull(grad)[0]


def contract(left, right, left_dim, right_dim):
    return lax.dot_general(
        left, right, (((left_dim,), (right_dim,)), ((), ())), preferred_element_type=jnp.float32
    )


def block_scores(query, key_block, query_pos, key_pos, scale):
    scores = (
        jnp.einsum("the,khe->htk", query, key_block, preferred_element_type=jnp.float32) * scale
    )
    allowed = key_pos[None, None, :] <= query_pos[None, :, None]
    return jnp.where(allowed, scores, NEG)


def matmul(left, right, left_dim, right_dim):
    return lax.dot_general(
        left, right, (((left_dim,), (right_dim,)), ((), ())), preferred_element_type=jnp.float32
    )


QUERY_ROWS = 256


def softmax_block(query, keys, values, first_query):
    scores = matmul(keys, query, 1, 1)
    key_pos = lax.broadcasted_iota(jnp.int32, scores.shape, 0)
    query_pos = lax.broadcasted_iota(jnp.int32, scores.shape, 1) + first_query
    scores = jnp.where(key_pos <= query_pos, scores, NEG)
    top = jnp.max(scores, axis=0, keepdims=True)
    weights = jnp.exp(scores - top)
    total = jnp.sum(weights, axis=0, keepdims=True)
    mixed = matmul(values, weights.astype(jnp.bfloat16), 0, 0) / total
    return mixed.astype(jnp.bfloat16), top + jnp.log(total)


def attend_kernel(place_ref, packed_ref, extra_ref, out_ref, outt_ref, lse_ref, xout_ref, xoutt_ref, xlse_ref):
    length = packed_ref.shape[0]
    scale = HEAD_DIM ** (-0.5)
    for start in range(0, length, QUERY_ROWS):
        stop = start + QUERY_ROWS
        query = packed_ref[start:stop, 0:64] * scale
        mixed, lse = softmax_block(
            query.astype(jnp.bfloat16), packed_ref[0:stop, 64:128], packed_ref[0:stop, 128:192], start
        )
        outt_ref[:, start:stop] = mixed
        out_ref[start:stop, :] = mixed.astype(jnp.float32).T.astype(jnp.bfloat16)
        lse_ref[:, start:stop] = lse
    query = (extra_ref[...] * scale).astype(jnp.bfloat16)
    mixed, lse = softmax_block(
        query, packed_ref[:, 192:256], packed_ref[:, 256:320], place_ref[0] * extra_ref.shape[0]
    )
    xoutt_ref[...] = mixed
    xout_ref[...] = mixed.astype(jnp.float32).T.astype(jnp.bfloat16)
    xlse_ref[...] = lse


def back_block(query, keys, values, lse, grad, mixed, first_query):
    scale = HEAD_DIM ** (-0.5)
    query = (query * scale).astype(jnp.bfloat16)
    scores = matmul(keys, query, 1, 1)
    key_pos = lax.broadcasted_iota(jnp.int32, scores.shape, 0)
    query_pos = lax.broadcasted_iota(jnp.int32, scores.shape, 1) + first_query
    prob = jnp.where(key_pos <= query_pos, jnp.exp(scores - lse), 0.0)
    grad_values = matmul(prob.astype(jnp.bfloat16), grad, 1, 0)
    grad_prob = matmul(values, grad, 1, 1)
    delta = jnp.sum(
        grad.astype(jnp.float32).T * mixed.astype(jnp.float32), axis=0, keepdims=True
    )
    grad_score = (prob * (grad_prob - delta)).astype(jnp.bfloat16)
    grad_keys = matmul(grad_score, query, 1, 0)
    grad_query = matmul(keys, grad_score, 0, 0) * scale
    return grad_query.T, grad_keys, grad_values


def attend_back_kernel(
    place_ref, packed_ref, extra_ref, outt_ref, lse_ref, xoutt_ref, xlse_ref, grad_ref, xgrad_ref,
    dpacked_ref, dextra_ref, dkeys, dvalues,
):
    length = packed_ref.shape[0]
    starts = list(range(0, length, QUERY_ROWS))
    for start in reversed(starts):
        stop = start + QUERY_ROWS
        dq, dk, dv = back_block(
            packed_ref[start:stop, 0:64], packed_ref[0:stop, 64:128], packed_ref[0:stop, 128:192],
            lse_ref[:, start:stop], grad_ref[start:stop, :], outt_ref[:, start:stop], start,
        )
        dpacked_ref[start:stop, 0:64] = dq.astype(jnp.bfloat16)
        if start == starts[-1]:
            dkeys[...] = dk
            dvalues[...] = dv
        else:
            dkeys[0:stop, :] += dk
            dvalues[0:stop, :] += dv
    dpacked_ref[:, 64:128] = dkeys[...].astype(jnp.bfloat16)
    dpacked_ref[:, 128:192] = dvalues[...].astype(jnp.bfloat16)
    dq, dk, dv = back_block(
        extra_ref[...], packed_ref[:, 192:256], packed_ref[:, 256:320],
        xlse_ref[...], xgrad_ref[...], xoutt_ref[...], place_ref[0] * extra_ref.shape[0],
    )
    dextra_ref[...] = dq.astype(jnp.bfloat16)
    dpacked_ref[:, 192:256] = dk.astype(jnp.bfloat16)
    dpacked_ref[:, 256:320] = dv.astype(jnp.bfloat16)


def vmem(count):
    return [pl.BlockSpec(memory_space=pltpu.VMEM)] * count


def attend(place, packed, extra):
    length, rows = packed.shape[0], extra.shape[0]
    bf16, f32 = jnp.bfloat16, jnp.float32
    return pl.pallas_call(
        attend_kernel,
        out_shape=(
            jax.ShapeDtypeStruct((length, HEAD_DIM), bf16),
            jax.ShapeDtypeStruct((HEAD_DIM, length), bf16),
            jax.ShapeDtypeStruct((1, length), f32),
            jax.ShapeDtypeStruct((rows, HEAD_DIM), bf16),
            jax.ShapeDtypeStruct((HEAD_DIM, rows), bf16),
            jax.ShapeDtypeStruct((1, rows), f32),
        ),
        in_specs=[pl.BlockSpec(memory_space=pltpu.SMEM)] + vmem(2),
        out_specs=tuple(vmem(6)),
        compiler_params=pltpu.CompilerParams(vmem_limit_bytes=40 * 2**20),
        name="attend",
    )(place, packed, extra)


def attend_back(place, packed, extra, outt, lse, xoutt, xlse, grad, xgrad):
    length, rows = packed.shape[0], extra.shape[0]
    return pl.pallas_call(
        attend_back_kernel,
        out_shape=(
            jax.ShapeDtypeStruct((length, 5 * HEAD_DIM), jnp.bfloat16),
            jax.ShapeDtypeStruct((rows, HEAD_DIM), jnp.bfloat16),
        ),
        in_specs=[pl.BlockSpec(memory_space=pltpu.SMEM)] + vmem(8),
        out_specs=tuple(vmem(2)),
        scratch_shapes=[
            pltpu.VMEM((length, HEAD_DIM), jnp.float32),
            pltpu.VMEM((length, HEAD_DIM), jnp.float32),
        ],
        compiler_params=pltpu.CompilerParams(vmem_limit_bytes=48 * 2**20),
        name="attend_back",
    )(place, packed, extra, outt, lse, xoutt, xlse, grad, xgrad)


def swap(blocks_of, axis):
    return lax.all_to_all(blocks_of, axis, split_axis=0, concat_axis=0, tiled=True)


def by_head(rows_of, blocks):
    return rows_of[:, : blocks * HEAD_DIM].reshape(-1, blocks, HEAD_DIM).transpose(1, 0, 2)


def from_head(parts, last):
    blocks, rows, _ = parts.shape
    return jnp.concatenate([parts.transpose(1, 0, 2).reshape(rows, blocks * HEAD_DIM), last], axis=1)


def head_attention(query, keys, values):
    blocks = lax.axis_size("ctx")
    rows = query.shape[0]
    place = lax.axis_index("ctx").astype(jnp.int32).reshape(1)
    cut = blocks * HEAD_DIM
    shared = jnp.concatenate([keys[:, cut:], values[:, cut:]], axis=1)
    packed = jnp.concatenate(
        [by_head(query, blocks), by_head(keys, blocks), by_head(values, blocks),
         jnp.broadcast_to(shared[None], (blocks, rows, 2 * HEAD_DIM))],
        axis=2,
    )
    packed = swap(packed, "ctx").reshape(blocks * rows, 5 * HEAD_DIM)
    extra = query[:, cut:]
    out, outt, lse, xout, xoutt, xlse = attend(place, packed, extra)
    back = swap(out.reshape(blocks, rows, HEAD_DIM), "ctx")
    joined = from_head(back, xout)

    def backward(grad_joined):
        grad = swap(by_head(grad_joined, blocks), "ctx").reshape(blocks * rows, HEAD_DIM)
        dpacked, dextra = attend_back(
            place, packed, extra, outt, lse, xoutt, xlse, grad, grad_joined[:, cut:]
        )
        dback = swap(dpacked.reshape(blocks, rows, 5 * HEAD_DIM), "ctx")
        dshared = jnp.sum(dback[:, :, 3 * HEAD_DIM :].astype(jnp.float32), axis=0).astype(jnp.bfloat16)
        return (
            from_head(dback[:, :, :HEAD_DIM], dextra),
            from_head(dback[:, :, HEAD_DIM : 2 * HEAD_DIM], dshared[:, :HEAD_DIM]),
            from_head(dback[:, :, 2 * HEAD_DIM : 3 * HEAD_DIM], dshared[:, HEAD_DIM:]),
        )

    return joined, backward


def ring_attention(query, keys, values):
    position = lax.axis_index("ctx")
    blocks = lax.axis_size("ctx")
    count_rows, width = query.shape
    scale = HEAD_DIM ** (-0.5)
    offsets = jnp.arange(count_rows, dtype=jnp.int32)
    query_pos = position * count_rows + offsets
    shape_heads = (count_rows, HEADS, HEAD_DIM)
    query, keys, values = (part.reshape(shape_heads) for part in (query, keys, values))

    def forward_block(carry, key_block, value_block, source):
        run_max, run_sum, accum = carry
        scores = block_scores(query, key_block, query_pos, source * count_rows + offsets, scale)
        new_max = jnp.maximum(run_max, jnp.max(scores, axis=-1))
        factor = jnp.exp(run_max - new_max)
        weights = jnp.exp(scores - new_max[:, :, None])
        run_sum = run_sum * factor + jnp.sum(weights, axis=-1)
        accum = accum * factor[:, :, None] + jnp.einsum(
            "htk,khe->hte",
            weights.astype(jnp.bfloat16),
            value_block,
            preferred_element_type=jnp.float32,
        )
        return (new_max, run_sum, accum)

    def forward_visit(step, state):
        carry, key_block, value_block, stored = state
        source = (position - step) % blocks
        carry = lax.cond(
            source <= position,
            lambda inner: forward_block(inner, key_block, value_block, source),
            lambda inner: inner,
            carry,
        )
        return (carry, key_block, value_block, stored)

    def forward_step(step, state):
        carry, key_block, value_block, stored = forward_visit(step, state)
        key_block, value_block = shifted((key_block, value_block), "ctx", 1)
        return (carry, key_block, value_block, stored)

    stored_start = ()
    start = (
        jnp.full((HEADS, count_rows), NEG, jnp.float32),
        jnp.zeros((HEADS, count_rows), jnp.float32),
        jnp.zeros((HEADS, count_rows, HEAD_DIM), jnp.float32),
    )
    state = lax.fori_loop(0, blocks - 1, forward_step, (start, keys, values, stored_start))
    (run_max, run_sum, accum), _, _, stored_blocks = forward_visit(blocks - 1, state)
    attended = (accum / run_sum[:, :, None]).transpose(1, 0, 2).astype(jnp.bfloat16)
    lse = run_max + jnp.log(run_sum)

    def backward(grad_joined):
        grad_attended = grad_joined.reshape(shape_heads)
        delta_rows = jnp.sum(
            grad_attended.astype(jnp.float32) * attended.astype(jnp.float32), axis=-1
        ).T

        def backward_block(source, key_block, value_block, grads):
            grad_query, grad_keys, grad_values = grads
            scores = block_scores(query, key_block, query_pos, source * count_rows + offsets, scale)
            prob = jnp.exp(scores - lse[:, :, None])
            grad_values = grad_values + jnp.einsum(
                "htk,the->khe",
                prob.astype(jnp.bfloat16),
                grad_attended,
                preferred_element_type=jnp.float32,
            )
            grad_prob = jnp.einsum(
                "the,khe->htk", grad_attended, value_block, preferred_element_type=jnp.float32
            )
            grad_score = (prob * (grad_prob - delta_rows[:, :, None]) * scale).astype(jnp.bfloat16)
            grad_query = grad_query + jnp.einsum(
                "htk,khe->the", grad_score, key_block, preferred_element_type=jnp.float32
            )
            grad_keys = grad_keys + jnp.einsum(
                "htk,the->khe", grad_score, query, preferred_element_type=jnp.float32
            )
            return (grad_query, grad_keys, grad_values)

        zero_block = jnp.zeros(shape_heads, jnp.float32)

        def backward_step(step, state):
            grad_query, key_block, value_block, grad_keys, grad_values = state
            source = (position - step) % blocks
            grad_query, grad_keys, grad_values = lax.cond(
                source <= position,
                lambda inner: backward_block(source, key_block, value_block, inner),
                lambda inner: inner,
                (grad_query, grad_keys, grad_values),
            )
            key_block, value_block = shifted((key_block, value_block), "ctx", 1)
            grad_keys, grad_values = from_behind((grad_keys, grad_values), "ctx", 1)
            return (grad_query, key_block, value_block, grad_keys, grad_values)

        grad_query, _, _, grad_keys, grad_values = lax.fori_loop(
            0, blocks, backward_step, (zero_block, keys, values, zero_block, zero_block)
        )
        return tuple(
            part.reshape(count_rows, width) for part in (grad_query, grad_keys, grad_values)
        )

    return attended.reshape(count_rows, width), backward


def other_half(value):
    return lax.ppermute(value, "fsdp", [(0, 1), (1, 0)])


def partner(value, bit):
    count = lax.axis_size("ctx")
    return lax.ppermute(value, "ctx", [(source, source ^ bit) for source in range(count)])


def after(value, earlier):
    return lax.optimization_barrier((value, earlier))[0]


def gather_weights(shards):
    quarter = lax.axis_index("ctx") % 4
    place = lax.axis_index("fsdp")
    wholes, earlier = [], None
    for shard in shards:
        depth, columns = shard.shape
        parts = shard.reshape(4, depth // 4, columns)
        piece = lax.dynamic_slice_in_dim(parts, quarter, 1, 0)
        if earlier is not None:
            piece = after(piece, earlier)
        first = other_half(piece)
        earlier = first
        second = partner(first, 2)
        third = partner(first, 1)
        fourth = partner(second, 1)
        whole = jnp.concatenate([parts, parts], axis=0)
        base = (1 - place) * 4
        for got, bits in ((first, 0), (second, 2), (third, 1), (fourth, 3)):
            whole = lax.dynamic_update_slice_in_dim(whole, got, base + (quarter ^ bits), 0)
        wholes.append(whole.reshape(2 * depth, columns))
    return wholes


def on_device(
    block_input,
    cotangent,
    first_gain,
    first_shift,
    qkv_weight,
    query_bias,
    value_bias,
    out_weight,
    out_bias,
    second_gain,
    second_shift,
    up_weight,
    up_bias,
    down_weight,
    down_bias,
):
    fsdp = lax.axis_size("fsdp")
    blocks = lax.axis_size("ctx")
    place = lax.axis_index("fsdp")
    width = HEADS * HEAD_DIM
    f32, bf16 = jnp.float32, jnp.bfloat16
    small = (
        first_gain, first_shift, query_bias, value_bias, out_bias, second_gain, second_shift,
        down_bias, up_bias,
    )
    sizes = [part.shape[0] for part in small]
    gathered = lax.all_gather(jnp.concatenate(small), "fsdp", axis=0, tiled=False)
    whole_small, at = [], 0
    for size in sizes:
        whole_small.append(gathered[:, at : at + size].reshape(fsdp * size).astype(f32))
        at += size
    gain_one, shift_one, bias_q, bias_v, bias_o, gain_two, shift_two, bias_d, bias_u = whole_small
    shards = (qkv_weight, out_weight, up_weight, down_weight)
    paired = fsdp == 2 and blocks % 4 == 0
    if paired:
        whole_qkv, whole_out, whole_up, whole_down = gather_weights(shards)
    else:
        whole_qkv, whole_out, whole_up, whole_down = (
            lax.all_gather(part, "fsdp", axis=0, tiled=True) for part in shards
        )
    rows = block_input.astype(f32)
    first_norm, first_hat, first_rstd = normalize(rows, gain_one, shift_one)
    first_act = first_norm.astype(bf16)
    qkv = jnp.dot(first_act, whole_qkv, preferred_element_type=f32)
    query = (qkv[:, :width] + bias_q).astype(bf16)
    keys = qkv[:, width : 2 * width].astype(bf16)
    values = (qkv[:, 2 * width :] + bias_v).astype(bf16)
    attention = head_attention if HEADS == blocks + 1 else ring_attention
    joined, attention_back = attention(query, keys, values)
    mid = rows + jnp.dot(joined, whole_out, preferred_element_type=f32) + bias_o
    second_norm, second_hat, second_rstd = normalize(mid, gain_two, shift_two)
    second_act = second_norm.astype(bf16)
    pre = jnp.dot(second_act, whole_up, preferred_element_type=f32) + bias_u
    act = gelu_tanh(pre).astype(bf16)
    block_output = mid + jnp.dot(act, whole_down, preferred_element_type=f32) + bias_d

    def left(part):
        if paired:
            half = part.shape[1] // 2
            own = lax.dynamic_slice_in_dim(part, place * half, half, 1)
            sent = lax.dynamic_slice_in_dim(part, (1 - place) * half, half, 1)
            return jnp.concatenate([own, other_half(sent)], axis=0)
        return lax.all_to_all(part, "fsdp", split_axis=1, concat_axis=0, tiled=True)

    def right(part):
        if paired:
            return jnp.concatenate([part, other_half(part)], axis=0)
        return lax.all_gather(part, "fsdp", axis=0, tiled=True)

    def weight_grad(left_part, right_part):
        return contract(left(left_part), right(right_part), 0, 0).astype(bf16)

    cot_float = cotangent.astype(f32)
    grad_down = weight_grad(act, cotangent)
    grad_down_bias = jnp.sum(cot_float, axis=0)
    grad_pre = gelu_back(pre, contract(cotangent, whole_down, 1, 1))
    grad_pre_b = grad_pre.astype(bf16)
    grad_up = weight_grad(second_act, grad_pre_b)
    grad_up_bias = jnp.sum(grad_pre, axis=0)
    grad_second = contract(grad_pre_b, whole_up, 1, 1)
    grad_second_gain = jnp.sum(grad_second * second_hat, axis=0)
    grad_second_shift = jnp.sum(grad_second, axis=0)
    grad_mid = cot_float + normalize_back(grad_second, second_hat, second_rstd, gain_two)
    grad_mid_b = grad_mid.astype(bf16)
    grad_out = weight_grad(joined, grad_mid_b)
    grad_out_bias = jnp.sum(grad_mid, axis=0)
    grad_attended = contract(grad_mid_b, whole_out, 1, 1).astype(bf16)
    grad_query, grad_keys, grad_values = attention_back(grad_attended)
    grad_query_bias = jnp.sum(grad_query.astype(f32), axis=0)
    grad_value_bias = jnp.sum(grad_values.astype(f32), axis=0)
    grad_qkv_b = jnp.concatenate([grad_query, grad_keys, grad_values], axis=1).astype(bf16)
    grad_qkv = weight_grad(first_act, grad_qkv_b)
    grad_first = contract(grad_qkv_b, whole_qkv, 1, 1)
    grad_first_gain = jnp.sum(grad_first * first_hat, axis=0)
    grad_first_shift = jnp.sum(grad_first, axis=0)
    input_grad = grad_mid + normalize_back(grad_first, first_hat, first_rstd, gain_one)
    vectors = (
        grad_first_gain, grad_first_shift, grad_query_bias, grad_value_bias, grad_out_bias,
        grad_second_gain, grad_second_shift, grad_down_bias, grad_up_bias,
    )
    packed_vectors = jnp.concatenate([part.reshape(fsdp, -1) for part in vectors], axis=1)
    mine = lax.dynamic_index_in_dim(packed_vectors, place, 0, keepdims=False)
    if paired:
        sent = lax.dynamic_index_in_dim(packed_vectors, 1 - place, 0, keepdims=False)
        mine = mine + other_half(sent)
    else:
        mine = lax.psum_scatter(packed_vectors, "fsdp", scatter_dimension=0, tiled=True)[0]
    depth, columns = grad_qkv.shape
    spare = -(-mine.shape[0] // (8 * columns)) * 8
    below = jnp.pad(mine.astype(bf16), (0, spare * columns - mine.shape[0]))
    grad_qkv = jnp.concatenate([grad_qkv, below.reshape(spare, columns)], axis=0)
    grad_qkv, grad_out, grad_up, grad_down = lax.psum(
        (grad_qkv, grad_out, grad_up, grad_down), "ctx"
    )
    mine = grad_qkv[depth:].reshape(-1).astype(f32)
    grad_qkv = grad_qkv[:depth]
    shards, at = [], 0
    for size in sizes:
        shards.append(mine[at : at + size])
        at += size
    gain_g1, shift_g1, bias_gq, bias_gv, bias_go, gain_g2, shift_g2, bias_gd, bias_gu = shards
    return (
        block_output,
        input_grad,
        gain_g1,
        shift_g1,
        grad_qkv.astype(f32),
        bias_gq,
        bias_gv,
        grad_out.astype(f32),
        bias_go,
        gain_g2,
        shift_g2,
        grad_up.astype(f32),
        bias_gu,
        grad_down.astype(f32),
        bias_gd,
    )


def solution(mesh):
    placed = (
        P(("fsdp", "ctx"), None),
        P(("fsdp", "ctx"), None),
        P("fsdp"),
        P("fsdp"),
        P("fsdp", None),
        P("fsdp"),
        P("fsdp"),
        P("fsdp", None),
        P("fsdp"),
        P("fsdp"),
        P("fsdp"),
        P("fsdp", None),
        P("fsdp"),
        P("fsdp", None),
        P("fsdp"),
    )
    return jax.shard_map(
        on_device,
        mesh=mesh,
        in_specs=placed,
        out_specs=(
            P(("fsdp", "ctx"), None),
            P(("fsdp", "ctx"), None),
            P("fsdp"),
            P("fsdp"),
            P("fsdp", None),
            P("fsdp"),
            P("fsdp"),
            P("fsdp", None),
            P("fsdp"),
            P("fsdp"),
            P("fsdp"),
            P("fsdp", None),
            P("fsdp"),
            P("fsdp", None),
            P("fsdp"),
        ),
        check_vma=False,
    )
```
